32 devices in a mesh: orb: 4 (over y, x), dom: 8 (over z, core).
Axes of the slice: x: 2, y: 2, z: 4, core: 2. Of those that a mesh axis runs over, the one named last changes fastest.
Arguments:
- orbitals: float32 [8, 40, 32, 128], P('orb', 'dom'), may hold values from -8 to 8
- face_metric: float32 [3, 40, 32, 128], P(None, 'dom'), may hold values from 0.2 to 2.2
- cross_metric: float32 [3, 40, 32, 128], P(None, 'dom'), may hold values from -0.25 to 0.25
- screen: float32 [40, 32, 128], P('dom'), may hold values from 0.1 to 0.4
- turn_orbital: int32 [4], replicated, may hold values from 0 to 7, as said below
Outputs:
- exchange: float32 [8, 40, 32, 128], P('orb', 'dom')
The draws below stay inside these ranges and needn't reach their ends.
Inputs may be any that keep to these rules, and one draw needn't show every extreme that they name: `turn_orbital`: orbital numbers; both 0 and 7 occur, and a number may recur.
All inputs are finite; a program needn't handle non-finite values.
Results may differ from the reference program's by a relative error of at most 0.0001.
Values sent between devices are 32-bit elements; how exact they have to be, the bound alone decides.
No kernel may reach another device: no remote copies, remote signals or barrier semaphores. Data moves between devices by JAX's collectives and lax.ppermute only.
A program may use at most 64 MiB of HBM per device.

```python
import math
import jax
import jax.numpy as jnp
from jax import lax

TURNS = 4
SWEEPS = 6
NY = 32
NZ = 128
ORBS = 8
NX = 40


def draw_turn_orbital(key, part):
    first_key, second_key = jax.random.split(jax.random.fold_in(key, 17))
    extra = jax.random.randint(first_key, (TURNS - 2,), 0, ORBS, dtype=jnp.int32)
    values = jnp.concatenate([jnp.array([0, ORBS - 1], dtype=jnp.int32), extra])
    order = jax.random.permutation(second_key, TURNS)
    return values[order].astype(jnp.int32)


def draw_face_metric(key, part):
    first_key, second_key = jax.random.split(jax.random.fold_in(key, 23))
    along_x = jnp.exp(jax.random.uniform(first_key, (1, NX, NY, NZ), jnp.float32, math.log(1.1), math.log(2.2)))
    across = jnp.exp(jax.random.uniform(second_key, (2, NX, NY, NZ), jnp.float32, math.log(0.2), math.log(0.4)))
    along_x = jnp.clip(along_x, 0.2, 2.2)
    across = jnp.clip(across, 0.2, 2.2)
    return jnp.concatenate([along_x, across], axis=0).astype(jnp.float32)


def draw_cross_metric(key, part):
    cross_key = jax.random.fold_in(key, 29)
    values = jax.random.uniform(cross_key, (3, NX, NY, NZ), jnp.float32, -0.25, 0.25)
    return values.astype(jnp.float32)


def draw_screen(key, part):
    screen_key = jax.random.fold_in(key, 31)
    values = jnp.exp(jax.random.uniform(screen_key, (NX, NY, NZ), jnp.float32, math.log(0.1), math.log(0.4)))
    return jnp.clip(values, 0.1, 0.4).astype(jnp.float32)


def shard_levels(key, dims, pieces, smallest, top_value):
    factor_of = 1.0
    for axis_at, shards_of in pieces:
        steps = jax.random.uniform(jax.random.fold_in(jax.random.fold_in(key, 6), axis_at), (shards_of,), jnp.float32, smallest / len(pieces), top_value / len(pieces))
        factor_of = factor_of * jnp.repeat(jnp.exp(steps), dims[axis_at] // shards_of).reshape((-1,) + (1,) * (len(dims) - 1 - axis_at))
    return factor_of


def centred(own_key, shape, spread, reach, cuts=(), kind=jnp.bfloat16):
    drawn = spread * jax.random.normal(own_key, shape, jnp.float32)
    if cuts:
        drawn = drawn * shard_levels(own_key, shape, cuts, -0.22, 0.18)
    return jnp.clip(drawn, -reach, reach).astype(kind)


def setup_inputs(seed: int = 0) -> dict:
    streams_of = jax.random.split(jax.random.key(seed), 6)
    orbitals = centred(streams_of[0], (ORBS, NX, NY, NZ), 1.5, 8.0, ((0, 4), (1, 8)), jnp.float32)
    face_metric = draw_face_metric(jax.random.fold_in(streams_of[5], 71), 0)
    cross_metric = draw_cross_metric(jax.random.fold_in(streams_of[5], 71), 0)
    screen = draw_screen(jax.random.fold_in(streams_of[5], 71), 0)
    turn_orbital = draw_turn_orbital(jax.random.fold_in(streams_of[5], 71), 0)
    return {"orbitals": orbitals, "face_metric": face_metric, "cross_metric": cross_metric, "screen": screen, "turn_orbital": turn_orbital}


def shifted(padded, along_x, along_y, along_z):
    cells_x = padded.shape[1] - 2
    cells_y = padded.shape[2] - 2
    cells_z = padded.shape[3] - 2
    return padded[:, 1 + along_x:1 + along_x + cells_x, 1 + along_y:1 + along_y + cells_y, 1 + along_z:1 + along_z + cells_z]


def coupled(padded, face, cross):
    total = face[0] * (shifted(padded, 1, 0, 0) + shifted(padded, -1, 0, 0))
    total = total + face[1] * (shifted(padded, 0, 1, 0) + shifted(padded, 0, -1, 0))
    total = total + face[2] * (shifted(padded, 0, 0, 1) + shifted(padded, 0, 0, -1))
    total = total + 0.25 * cross[0] * (shifted(padded, 1, 1, 0) + shifted(padded, -1, -1, 0) - shifted(padded, 1, -1, 0) - shifted(padded, -1, 1, 0))
    total = total + 0.25 * cross[1] * (shifted(padded, 1, 0, 1) + shifted(padded, -1, 0, -1) - shifted(padded, 1, 0, -1) - shifted(padded, -1, 0, 1))
    total = total + 0.25 * cross[2] * (shifted(padded, 0, 1, 1) + shifted(padded, 0, -1, -1) - shifted(padded, 0, 1, -1) - shifted(padded, 0, -1, 1))
    return total


def diagonal_inverse(face, cross, screen):
    diag = screen + 2.0 * (face[0] + face[1] + face[2]) + (jnp.abs(cross[0]) + jnp.abs(cross[1]) + jnp.abs(cross[2]))
    return 1.0 / diag


def reference(orbitals, face_metric, cross_metric, screen, turn_orbital):
    inverse = diagonal_inverse(face_metric, cross_metric, screen)
    result = jnp.zeros_like(orbitals)
    numbers = jnp.arange(ORBS, dtype=jnp.int32)
    for turn_index in range(TURNS):
        which = turn_orbital[turn_index].astype(jnp.int32)
        chosen = lax.dynamic_index_in_dim(orbitals, which, 0, keepdims=True)

        def solve_one(orbital):
            density = orbital[None] * chosen
            iterate = density * inverse
            for sweep_index in range(SWEEPS - 1):
                padded = jnp.pad(iterate, ((0, 0), (1, 1), (1, 1), (1, 1)))
                iterate = (density + coupled(padded, face_metric, cross_metric)) * inverse
            return iterate[0]

        potentials = lax.map(solve_one, orbitals)
        result = result + potentials * chosen
        backward = jnp.sum(potentials * orbitals, axis=0)
        result = result + jnp.where((numbers == which)[:, None, None, None], backward[None], jnp.float32(0.0))
    return result
```

```python
import functools

import jax
import jax.numpy as jnp
from jax import lax
from jax.experimental import pallas as pl
from jax.experimental.pallas import tpu as pltpu
from jax.sharding import PartitionSpec as P

SWEEPS = 6
DEEP = SWEEPS - 1
BATCH = 4
LANES = 128
TOP = 7
TALL = 32
LIMIT = 24 * 1024 * 1024


def padded_to_tile(rows):
    return -(-rows // 8) * 8


class Sizes:
    def __init__(self, groups, mine, planes, height, turns):
        self.groups, self.mine, self.planes, self.turns = groups, mine, planes, turns
        self.height = height
        self.orbs = groups * mine
        self.rows = height // groups
        self.window = self.rows + 2 * DEEP
        self.inner = self.window - 2
        self.span = planes + 2 * DEEP
        self.edge = DEEP - 1
        self.orb_rows = mine * planes * self.window
        self.orb_pack = padded_to_tile(self.orb_rows)
        self.metric_at = DEEP * self.window
        self.orb_at = self.metric_at + 6 * self.edge * self.inner
        self.side_pack = padded_to_tile(self.orb_at + self.orb_rows)


def pack_kernel(sz, orb_ref, face_ref, cross_ref, screen_ref, *refs):
    pieces = refs[: sz.groups]
    far_ref, near_ref, inv_ref, met_ref, orb_pad, met_pad = refs[sz.groups :]
    group = lax.axis_index("orb")
    odd = lax.rem(lax.axis_index("dom"), 2)
    zeros = jnp.zeros((8, LANES), jnp.float32)
    end = 8 + sz.height
    for p in range(sz.planes):
        for j in range(sz.mine):
            orb_pad[j, p, 0:8] = zeros
            orb_pad[j, p, end : end + 8] = zeros
            orb_pad[j, p, 8:end] = orb_ref[j, p]
        diag = screen_ref[p] + 2.0 * (face_ref[0, p] + face_ref[1, p] + face_ref[2, p])
        diag = diag + (jnp.abs(cross_ref[0, p]) + jnp.abs(cross_ref[1, p]) + jnp.abs(cross_ref[2, p]))
        met_pad[6, p, 8:end] = 1.0 / diag
        for c in range(3):
            met_pad[c, p, 8:end] = face_ref[c, p]
            met_pad[3 + c, p, 8:end] = 0.25 * cross_ref[c, p]
        for c in range(7):
            met_pad[c, p, 0:8] = zeros
            met_pad[c, p, end : end + 8] = zeros
    own = 8 + group * sz.rows - DEEP
    for s in range(sz.groups):
        first = 8 + jnp.bitwise_xor(group, s) * sz.rows - DEEP
        for j in range(sz.mine):
            for p in range(sz.planes):
                at = (j * sz.planes + p) * sz.window
                pieces[s][at : at + sz.window] = orb_pad[j, p, pl.ds(first, sz.window)]
    for ref, from_end in ((far_ref, odd), (near_ref, 1 - odd)):
        first_inv = from_end * (sz.planes - DEEP)
        first_met = from_end * (sz.planes - sz.edge)
        for p in range(DEEP):
            at = p * sz.window
            ref[at : at + sz.window] = met_pad[6, first_inv + p, pl.ds(own, sz.window)]
        for c in range(6):
            for p in range(sz.edge):
                at = sz.metric_at + (c * sz.edge + p) * sz.inner
                ref[at : at + sz.inner] = met_pad[c, first_met + p, pl.ds(own + 1, sz.inner)]
        for j in range(sz.mine):
            for p in range(DEEP):
                at = sz.orb_at + (j * DEEP + p) * sz.window
                ref[at : at + sz.window] = orb_pad[j, first_inv + p, pl.ds(own, sz.window)]
    for p in range(sz.planes):
        inv_ref[p, 0 : sz.window] = met_pad[6, p, pl.ds(own, sz.window)]
        for c in range(6):
            met_ref[c, p, 0 : sz.inner] = met_pad[c, p, pl.ds(own + 1, sz.inner)]


def list_pairs(sz, group, turn_ref, first_ref, second_ref, weight_ref, seen_ref, mult_ref):
    def slot_of(k):
        return jnp.bitwise_xor(k // sz.mine, group) * sz.mine + lax.rem(k, sz.mine)

    for i in range(sz.orbs):
        seen_ref[i] = 0
        mult_ref[i] = 0
    slots = [slot_of(turn_ref[t]) for t in range(sz.turns)]
    for k in slots:
        mult_ref[k] = mult_ref[k] + 1
    count = jnp.int32(0)
    for k in slots:
        fresh = 1 - seen_ref[k]
        times = mult_ref[k]

        def step(i, count, k=k, fresh=fresh, times=times):
            first_ref[count] = k
            second_ref[count] = i
            weight_ref[count] = times + mult_ref[i]
            return count + fresh * (1 - seen_ref[i])

        count = lax.fori_loop(0, sz.orbs, step, count)
        seen_ref[k] = 1
    for i in range(BATCH):
        first_ref[count + i] = 0
        second_ref[count + i] = 0
        weight_ref[count + i] = 0
    return count


def relax_kernel(sz, turn_ref, *refs):
    gathered = refs[: sz.groups]
    far_ref, near_ref, far_rest, near_rest, inv_ref, met_ref = refs[sz.groups : sz.groups + 6]
    outs = refs[sz.groups + 6 : 2 * sz.groups + 6]
    orbs, inv, coef, start, ping, pong, total, first_ref, second_ref, weight_ref, seen_ref, mult_ref = refs[
        2 * sz.groups + 6 :
    ]
    group = lax.axis_index("orb")
    odd = lax.rem(lax.axis_index("dom"), 2)
    n, win = sz.planes, sz.window
    below, above = 0, n + DEEP
    far_at = jnp.where(odd == 1, above, below)
    near_at = jnp.where(odd == 1, below, above)
    zeros = jnp.zeros((8, LANES), jnp.float32)

    count = list_pairs(sz, group, turn_ref, first_ref, second_ref, weight_ref, seen_ref, mult_ref)

    if TOP + win < 25:
        for p in range(sz.span):
            for r in range(0, TALL, 8):
                inv[p, r : r + 8] = zeros
                for i in range(sz.orbs):
                    orbs[i, p, r : r + 8] = zeros
                if r < 16:
                    for c in range(6):
                        coef[c, p, r : r + 8] = zeros
    for p in range(n):
        inv[DEEP + p, TOP : TOP + win] = inv_ref[p, 0:win]
        for c in range(6):
            coef[c, DEEP + p, 0 : sz.inner] = met_ref[c, p, 0 : sz.inner]
        for s in range(sz.groups):
            for j in range(sz.mine):
                at = (j * n + p) * win
                orbs[s * sz.mine + j, DEEP + p, TOP : TOP + win] = gathered[s][at : at + win]
    for ref, rest, at in ((far_ref, far_rest, far_at), (near_ref, near_rest, near_at)):
        for p in range(DEEP):
            inv[at + p, TOP : TOP + win] = ref[p * win : (p + 1) * win]
            for j in range(sz.mine):
                row = sz.orb_at + (j * DEEP + p) * win
                orbs[j, at + p, TOP : TOP + win] = ref[row : row + win]
            for i in range(sz.orbs - sz.mine):
                row = (i // sz.mine) * sz.orb_pack + ((i % sz.mine) * n + p) * win
                orbs[sz.mine + i, at + p, TOP : TOP + win] = rest[row : row + win]
        met_first = at + jnp.where(at == 0, 1, 0)
        for c in range(6):
            for p in range(sz.edge):
                row = sz.metric_at + (c * sz.edge + p) * sz.inner
                coef[c, met_first + p, 0 : sz.inner] = ref[row : row + sz.inner]

    lane = lax.broadcasted_iota(jnp.int32, (8, LANES), 1)

    def prepare(p, carry):
        for r in (0, 8):
            scale = inv[p, 8 + r : 16 + r]
            fx, fy, fz, xy, xz, yz = [coef[c, p, r : r + 8] * scale for c in range(6)]
            coef[0, p, r : r + 8] = fx
            coef[1, p, r : r + 8] = fy
            coef[2, p, r : r + 8] = xy
            for at, values, sign in ((3, fz, 1.0), (4, xz, -1.0), (5, yz, -1.0)):
                up = jnp.where(lane == 0, 0.0, pltpu.roll(values, 1, 1))
                down = jnp.where(lane == LANES - 1, 0.0, pltpu.roll(values, LANES - 1, 1))
                coef[at, p, r : r + 8] = up
                coef[at + 3, p, r : r + 8] = sign * down
        return carry

    lax.fori_loop(1, sz.span - 1, prepare, 0)

    for f in range(BATCH):
        for p in range(sz.span):
            for buf in (ping, pong):
                buf[f, p, 0:8] = zeros
                buf[f, p, TALL - 8 : TALL] = zeros
    for i in range(sz.orbs):
        for p in range(n):
            total[i, p] = zeros

    def sweep(source, number, row, planes, put):
        values = {}

        def fetch(f, p):
            up = source[f, p, row + 1 : row + 9]
            down = source[f, p, row - 1 : row + 7]
            return source[f, p, row : row + 8], up - down, up + down

        for f in range(BATCH):
            values[f, planes[0] - 1] = fetch(f, planes[0] - 1)
            values[f, planes[0]] = fetch(f, planes[0])
        for p in planes:
            cs = [coef[c, p, row - 8 : row] for c in range(9)]
            for f in range(BATCH):
                values[f, p + 1] = fetch(f, p + 1)
                before, diff_before, _ = values.pop((f, p - 1))
                here, diff, both = values[f, p]
                after, diff_after, _ = values[f, p + 1]
                slope = after - before
                up = cs[3] * here + cs[4] * slope + cs[5] * diff
                down = cs[6] * here + cs[7] * slope + cs[8] * diff
                new = start[f, p, row : row + 8] + cs[0] * (after + before)
                new = new + cs[1] * both + cs[2] * (diff_after - diff_before)
                new = new + (pltpu.roll(up, LANES - 1, 1) + pltpu.roll(down, 1, 1))
                put(f, p, new)

    def batch(index, carry):
        base = index * BATCH
        firsts = [first_ref[base + f] for f in range(BATCH)]
        seconds = [second_ref[base + f] for f in range(BATCH)]
        for p in range(sz.span):
            for r, size in ((TOP, 8), (TOP + 8, 8), (TOP + 16, 2)):
                scale = inv[p, r : r + size]
                for f in range(BATCH):
                    start[f, p, r : r + size] = (
                        orbs[firsts[f], p, r : r + size] * orbs[seconds[f], p, r : r + size] * scale
                    )
        source = start
        for number in range(1, DEEP):
            target = ping if number % 2 else pong
            planes = list(range(number, sz.span - number))
            for row in (8, 16):

                def put(f, p, new, row=row, target=target):
                    target[f, p, row : row + 8] = new

                sweep(source, number, row, planes, put)
            source = target
        row = TOP + DEEP
        weights = []
        for f in range(BATCH):
            w = weight_ref[base + f]
            weights.append(
                (w.astype(jnp.float32), jnp.where(firsts[f] == seconds[f], 0, w).astype(jnp.float32))
            )

        def put(f, p, new):
            a, b = firsts[f], seconds[f]
            q = p - DEEP
            total[a, q] = total[a, q] + (weights[f][0] * new) * orbs[b, p, row : row + 8]
            total[b, q] = total[b, q] + (weights[f][1] * new) * orbs[a, p, row : row + 8]

        sweep(source, DEEP, row, list(range(DEEP, sz.span - DEEP)), put)
        return carry

    lax.fori_loop(0, (count + BATCH - 1) // BATCH, batch, 0)

    for s in range(sz.groups):
        for j in range(sz.mine):
            for p in range(n):
                outs[s][j, p] = total[s * sz.mine + j, p, 0 : sz.rows]


def unpack_kernel(sz, *refs):
    blocks, out_ref = refs[: sz.groups], refs[sz.groups]
    group = lax.axis_index("orb")
    for s in range(sz.groups):
        first = jnp.bitwise_xor(group, s) * sz.rows
        if sz.rows % 8 == 0:
            first = pl.multiple_of(first, 8)
        for j in range(sz.mine):
            for p in range(sz.planes):
                out_ref[j, p, pl.ds(first, sz.rows)] = blocks[s][j, p]


def body(groups, slabs, orbitals, face_metric, cross_metric, screen, turn_orbital):
    mine, planes, height, lanes = orbitals.shape
    sz = Sizes(groups, mine, planes, height, turn_orbital.shape[0])
    f32 = jnp.float32
    vmem = pl.BlockSpec(memory_space=pltpu.VMEM)
    smem = pl.BlockSpec(memory_space=pltpu.SMEM)
    params = pltpu.CompilerParams(vmem_limit_bytes=LIMIT)

    packed = pl.pallas_call(
        functools.partial(pack_kernel, sz),
        out_shape=[jax.ShapeDtypeStruct((sz.orb_pack, lanes), f32)] * groups
        + [jax.ShapeDtypeStruct((sz.side_pack, lanes), f32)] * 2
        + [
            jax.ShapeDtypeStruct((planes, 24, lanes), f32),
            jax.ShapeDtypeStruct((6, planes, 16, lanes), f32),
        ],
        in_specs=[vmem] * 4,
        out_specs=[vmem] * (groups + 4),
        scratch_shapes=[
            pltpu.VMEM((mine, planes, height + 16, lanes), f32),
            pltpu.VMEM((7, planes, height + 16, lanes), f32),
        ],
        compiler_params=params,
        name="pack",
    )(orbitals, face_metric, cross_metric, screen)
    pieces = packed[:groups]
    far, near, inverse, metric = packed[groups:]

    def swap(x, s):
        return lax.ppermute(x, "orb", [(i, i ^ s) for i in range(groups)])

    to_near = [(i, i ^ 1) for i in range(slabs)]
    to_far = [(i, ((i + 1) ^ 1) - 1) for i in range(1, slabs - 1)]
    gathered = [pieces[0]] + [swap(pieces[s], s) for s in range(1, groups)]
    far_side = lax.ppermute(far, "dom", to_far)
    near_side = lax.ppermute(near, "dom", to_near)
    rest = jnp.concatenate(gathered[1:], axis=0)
    far_rest = lax.ppermute(rest, "dom", to_far)
    near_rest = lax.ppermute(rest, "dom", to_near)

    room = sz.turns * sz.orbs + BATCH
    field = pltpu.VMEM((BATCH, sz.span, TALL, lanes), f32)
    shares = pl.pallas_call(
        functools.partial(relax_kernel, sz),
        out_shape=[jax.ShapeDtypeStruct((mine, planes, sz.rows, lanes), f32)] * groups,
        in_specs=[smem] + [vmem] * (groups + 6),
        out_specs=[vmem] * groups,
        scratch_shapes=[
            pltpu.VMEM((sz.orbs, sz.span, TALL, lanes), f32),
            pltpu.VMEM((sz.span, TALL, lanes), f32),
            pltpu.VMEM((9, sz.span, 16, lanes), f32),
            field,
            field,
            field,
            pltpu.VMEM((sz.orbs, planes, 8, lanes), f32),
            pltpu.SMEM((room,), jnp.int32),
            pltpu.SMEM((room,), jnp.int32),
            pltpu.SMEM((room,), jnp.int32),
            pltpu.SMEM((sz.orbs,), jnp.int32),
            pltpu.SMEM((sz.orbs,), jnp.int32),
        ],
        compiler_params=params,
        name="relax",
    )(turn_orbital, *gathered, far_side, near_side, far_rest, near_rest, inverse, metric)
    blocks = [shares[0]] + [swap(shares[s], s) for s in range(1, groups)]
    return pl.pallas_call(
        functools.partial(unpack_kernel, sz),
        out_shape=jax.ShapeDtypeStruct((mine, planes, height, lanes), f32),
        in_specs=[vmem] * groups,
        out_specs=vmem,
        compiler_params=params,
        name="unpack",
    )(*blocks)


def solution(mesh):
    in_specs = (
        P("orb", "dom", None, None),
        P(None, "dom", None, None),
        P(None, "dom", None, None),
        P("dom", None, None),
        P(),
    )
    out_specs = P("orb", "dom", None, None)
    return jax.shard_map(
        functools.partial(body, mesh.shape["orb"], mesh.shape["dom"]),
        mesh=mesh,
        in_specs=in_specs,
        out_specs=out_specs,
        check_vma=False,
    )
```

```python
import functools

import jax
import jax.numpy as jnp
from jax import lax
from jax.experimental import pallas as pl
from jax.experimental.pallas import tpu as pltpu
from jax.sharding import PartitionSpec as P

SWEEPS = 6
DEEP = SWEEPS - 1
BATCH = 4
LANES = 128
TOP = 7
TALL = 32
LIMIT = 24 * 1024 * 1024


def padded_to_tile(rows):
    return -(-rows // 8) * 8


class Sizes:
    def __init__(self, groups, mine, planes, height, turns):
        self.groups, self.mine, self.planes, self.turns = groups, mine, planes, turns
        self.height = height
        self.orbs = groups * mine
        self.rows = height // groups
        self.window = self.rows + 2 * DEEP
        self.inner = self.window - 2
        self.span = planes + 2 * DEEP
        self.edge = DEEP - 1
        self.orb_rows = mine * planes * self.window
        self.orb_pack = padded_to_tile(self.orb_rows)
        self.metric_at = DEEP * self.window
        self.orb_at = self.metric_at + 6 * self.edge * self.inner
        self.side_pack = padded_to_tile(self.orb_at + self.orb_rows)


def pack_kernel(sz, orb_in, face_in, cross_in, screen_in, *refs):
    pieces = refs[: sz.groups]
    far_ref, near_ref, inv_ref, met_ref, orb_pad, met_pad = refs[sz.groups : sz.groups + 6]
    orb_ref, face_ref, cross_ref, screen_ref, sems = refs[sz.groups + 6 :]
    copies = [
        pltpu.make_async_copy(source, target, sems.at[i])
        for i, (source, target) in enumerate(
            ((orb_in, orb_ref), (face_in, face_ref), (cross_in, cross_ref), (screen_in, screen_ref))
        )
    ]
    for copy in copies:
        copy.start()
    group = lax.axis_index("orb")
    odd = lax.rem(lax.axis_index("dom"), 2)
    zeros = jnp.zeros((8, LANES), jnp.float32)
    end = 8 + sz.height
    for copy in copies:
        copy.wait()
    for p in range(sz.planes):
        for j in range(sz.mine):
            orb_pad[j, p, 0:8] = zeros
            orb_pad[j, p, end : end + 8] = zeros
            orb_pad[j, p, 8:end] = orb_ref[j, p]
        diag = screen_ref[p] + 2.0 * (face_ref[0, p] + face_ref[1, p] + face_ref[2, p])
        diag = diag + (jnp.abs(cross_ref[0, p]) + jnp.abs(cross_ref[1, p]) + jnp.abs(cross_ref[2, p]))
        met_pad[6, p, 8:end] = 1.0 / diag
        for c in range(3):
            met_pad[c, p, 8:end] = face_ref[c, p]
            met_pad[3 + c, p, 8:end] = 0.25 * cross_ref[c, p]
        for c in range(7):
            met_pad[c, p, 0:8] = zeros
            met_pad[c, p, end : end + 8] = zeros
    own = 8 + group * sz.rows - DEEP
    for s in range(sz.groups):
        first = 8 + jnp.bitwise_xor(group, s) * sz.rows - DEEP
        for j in range(sz.mine):
            for p in range(sz.planes):
                at = (j * sz.planes + p) * sz.window
                pieces[s][at : at + sz.window] = orb_pad[j, p, pl.ds(first, sz.window)]
    for ref, from_end in ((far_ref, odd), (near_ref, 1 - odd)):
        first_inv = from_end * (sz.planes - DEEP)
        first_met = from_end * (sz.planes - sz.edge)
        for p in range(DEEP):
            at = p * sz.window
            ref[at : at + sz.window] = met_pad[6, first_inv + p, pl.ds(own, sz.window)]
        for c in range(6):
            for p in range(sz.edge):
                at = sz.metric_at + (c * sz.edge + p) * sz.inner
                ref[at : at + sz.inner] = met_pad[c, first_met + p, pl.ds(own + 1, sz.inner)]
        for j in range(sz.mine):
            for p in range(DEEP):
                at = sz.orb_at + (j * DEEP + p) * sz.window
                ref[at : at + sz.window] = orb_pad[j, first_inv + p, pl.ds(own, sz.window)]
    for p in range(sz.planes):
        inv_ref[p, 0 : sz.window] = met_pad[6, p, pl.ds(own, sz.window)]
        for c in range(6):
            met_ref[c, p, 0 : sz.inner] = met_pad[c, p, pl.ds(own + 1, sz.inner)]


def list_pairs(sz, group, turn_ref, first_ref, second_ref, weight_ref, seen_ref, mult_ref):
    def slot_of(k):
        return jnp.bitwise_xor(k // sz.mine, group) * sz.mine + lax.rem(k, sz.mine)

    for i in range(sz.orbs):
        seen_ref[i] = 0
        mult_ref[i] = 0
    slots = [slot_of(turn_ref[t]) for t in range(sz.turns)]
    for k in slots:
        mult_ref[k] = mult_ref[k] + 1
    count = jnp.int32(0)
    for k in slots:
        fresh = 1 - seen_ref[k]
        times = mult_ref[k]

        def step(i, count, k=k, fresh=fresh, times=times):
            first_ref[count] = k
            second_ref[count] = i
            weight_ref[count] = times + mult_ref[i]
            return count + fresh * (1 - seen_ref[i])

        count = lax.fori_loop(0, sz.orbs, step, count)
        seen_ref[k] = 1
    for i in range(BATCH):
        first_ref[count + i] = 0
        second_ref[count + i] = 0
        weight_ref[count + i] = 0
    return count


def relax_kernel(sz, slabs, turn_in, *refs):
    gathered = refs[: sz.groups]
    far_ref, near_ref, far_rest, near_rest, inv_ref, met_ref = refs[sz.groups : sz.groups + 6]
    outs = refs[sz.groups + 6 : 2 * sz.groups + 6]
    orbs, inv, coef, start, ping, pong, total, first_ref, second_ref, weight_ref, seen_ref, mult_ref, turn_ref, sem = (
        refs[2 * sz.groups + 6 :]
    )
    turns = pltpu.make_async_copy(turn_in, turn_ref, sem)
    turns.start()
    group = lax.axis_index("orb")
    slab = lax.axis_index("dom")
    odd = lax.rem(slab, 2)
    inside = jnp.where((slab == 0) | (slab == slabs - 1), 0.0, 1.0)
    n, win = sz.planes, sz.window
    below, above = 0, n + DEEP
    far_at = jnp.where(odd == 1, above, below)
    near_at = jnp.where(odd == 1, below, above)
    zeros = jnp.zeros((8, LANES), jnp.float32)

    if TOP + win < 25:
        for p in range(sz.span):
            for r in range(0, TALL, 8):
                inv[p, r : r + 8] = zeros
                for i in range(sz.orbs):
                    orbs[i, p, r : r + 8] = zeros
                if r < 16:
                    for c in range(6):
                        coef[c, p, r : r + 8] = zeros
    for p in range(n):
        inv[DEEP + p, TOP : TOP + win] = inv_ref[p, 0:win]
        for c in range(6):
            coef[c, DEEP + p, 0 : sz.inner] = met_ref[c, p, 0 : sz.inner]
        for s in range(sz.groups):
            for j in range(sz.mine):
                at = (j * n + p) * win
                orbs[s * sz.mine + j, DEEP + p, TOP : TOP + win] = gathered[s][at : at + win]
    for ref, rest, at, live in ((far_ref, far_rest, far_at, inside), (near_ref, near_rest, near_at, None)):

        def kept(values, live=live):
            return values if live is None else values * live

        for p in range(DEEP):
            inv[at + p, TOP : TOP + win] = kept(ref[p * win : (p + 1) * win])
            for j in range(sz.mine):
                row = sz.orb_at + (j * DEEP + p) * win
                orbs[j, at + p, TOP : TOP + win] = kept(ref[row : row + win])
            for i in range(sz.orbs - sz.mine):
                row = (i // sz.mine) * sz.orb_pack + ((i % sz.mine) * n + p) * win
                orbs[sz.mine + i, at + p, TOP : TOP + win] = kept(rest[row : row + win])
        met_first = at + jnp.where(at == 0, 1, 0)
        for c in range(6):
            for p in range(sz.edge):
                row = sz.metric_at + (c * sz.edge + p) * sz.inner
                coef[c, met_first + p, 0 : sz.inner] = kept(ref[row : row + sz.inner])

    lane = lax.broadcasted_iota(jnp.int32, (8, LANES), 1)

    def prepare(p, carry):
        for r in (0, 8):
            scale = inv[p, 8 + r : 16 + r]
            fx, fy, fz, xy, xz, yz = [coef[c, p, r : r + 8] * scale for c in range(6)]
            coef[0, p, r : r + 8] = fx
            coef[1, p, r : r + 8] = fy
            coef[2, p, r : r + 8] = xy
            for at, values, sign in ((3, fz, 1.0), (4, xz, -1.0), (5, yz, -1.0)):
                up = jnp.where(lane == 0, 0.0, pltpu.roll(values, 1, 1))
                down = jnp.where(lane == LANES - 1, 0.0, pltpu.roll(values, LANES - 1, 1))
                coef[at, p, r : r + 8] = up
                coef[at + 3, p, r : r + 8] = sign * down
        return carry

    lax.fori_loop(1, sz.span - 1, prepare, 0)

    for f in range(BATCH):
        for p in range(sz.span):
            for buf in (ping, pong):
                buf[f, p, 0:8] = zeros
                buf[f, p, TALL - 8 : TALL] = zeros
    for i in range(sz.orbs):
        for p in range(n):
            total[i, p] = zeros
    turns.wait()
    count = list_pairs(sz, group, turn_ref, first_ref, second_ref, weight_ref, seen_ref, mult_ref)

    def sweep(source, number, row, planes, put):
        values = {}

        def fetch(f, p):
            up = source[f, p, row + 1 : row + 9]
            down = source[f, p, row - 1 : row + 7]
            return source[f, p, row : row + 8], up - down, up + down

        for f in range(BATCH):
            values[f, planes[0] - 1] = fetch(f, planes[0] - 1)
            values[f, planes[0]] = fetch(f, planes[0])
        for p in planes:
            cs = [coef[c, p, row - 8 : row] for c in range(9)]
            for f in range(BATCH):
                values[f, p + 1] = fetch(f, p + 1)
                before, diff_before, _ = values.pop((f, p - 1))
                here, diff, both = values[f, p]
                after, diff_after, _ = values[f, p + 1]
                slope = after - before
                up = cs[3] * here + cs[4] * slope + cs[5] * diff
                down = cs[6] * here + cs[7] * slope + cs[8] * diff
                new = start[f, p, row : row + 8] + cs[0] * (after + before)
                new = new + cs[1] * both + cs[2] * (diff_after - diff_before)
                new = new + (pltpu.roll(up, LANES - 1, 1) + pltpu.roll(down, 1, 1))
                put(f, p, new)

    def batch(index, carry):
        base = index * BATCH
        firsts = [first_ref[base + f] for f in range(BATCH)]
        seconds = [second_ref[base + f] for f in range(BATCH)]
        for p in range(sz.span):
            for r, size in ((TOP, 8), (TOP + 8, 8), (TOP + 16, 2)):
                scale = inv[p, r : r + size]
                for f in range(BATCH):
                    start[f, p, r : r + size] = (
                        orbs[firsts[f], p, r : r + size] * orbs[seconds[f], p, r : r + size] * scale
                    )
        source = start
        for number in range(1, DEEP):
            target = ping if number % 2 else pong
            planes = list(range(number, sz.span - number))
            for row in (8, 16):

                def put(f, p, new, row=row, target=target):
                    target[f, p, row : row + 8] = new

                sweep(source, number, row, planes, put)
            source = target
        row = TOP + DEEP
        weights = []
        for f in range(BATCH):
            w = weight_ref[base + f]
            weights.append(
                (w.astype(jnp.float32), jnp.where(firsts[f] == seconds[f], 0, w).astype(jnp.float32))
            )

        def put(f, p, new):
            a, b = firsts[f], seconds[f]
            q = p - DEEP
            total[a, q] = total[a, q] + (weights[f][0] * new) * orbs[b, p, row : row + 8]
            total[b, q] = total[b, q] + (weights[f][1] * new) * orbs[a, p, row : row + 8]

        sweep(source, DEEP, row, list(range(DEEP, sz.span - DEEP)), put)
        return carry

    lax.fori_loop(0, (count + BATCH - 1) // BATCH, batch, 0)

    for s in range(sz.groups):
        for j in range(sz.mine):
            for p in range(n):
                outs[s][j, p] = total[s * sz.mine + j, p, 0 : sz.rows]


def unpack_kernel(sz, *refs):
    blocks, out_ref = refs[: sz.groups], refs[sz.groups]
    group = lax.axis_index("orb")
    for s in range(sz.groups):
        first = jnp.bitwise_xor(group, s) * sz.rows
        if sz.rows % 8 == 0:
            first = pl.multiple_of(first, 8)
        for j in range(sz.mine):
            for p in range(sz.planes):
                out_ref[j, p, pl.ds(first, sz.rows)] = blocks[s][j, p]


def body(groups, slabs, orbitals, face_metric, cross_metric, screen, turn_orbital):
    mine, planes, height, lanes = orbitals.shape
    sz = Sizes(groups, mine, planes, height, turn_orbital.shape[0])
    f32 = jnp.float32
    vmem = pl.BlockSpec(memory_space=pltpu.VMEM)
    hbm = pl.BlockSpec(memory_space=pltpu.HBM)
    params = pltpu.CompilerParams(vmem_limit_bytes=LIMIT)

    packed = pl.pallas_call(
        functools.partial(pack_kernel, sz),
        out_shape=[jax.ShapeDtypeStruct((sz.orb_pack, lanes), f32)] * groups
        + [jax.ShapeDtypeStruct((sz.side_pack, lanes), f32)] * 2
        + [
            jax.ShapeDtypeStruct((planes, 24, lanes), f32),
            jax.ShapeDtypeStruct((6, planes, 16, lanes), f32),
        ],
        in_specs=[hbm] * 4,
        out_specs=[vmem] * (groups + 4),
        scratch_shapes=[
            pltpu.VMEM((mine, planes, height + 16, lanes), f32),
            pltpu.VMEM((7, planes, height + 16, lanes), f32),
            pltpu.VMEM((mine, planes, height, lanes), f32),
            pltpu.VMEM((3, planes, height, lanes), f32),
            pltpu.VMEM((3, planes, height, lanes), f32),
            pltpu.VMEM((planes, height, lanes), f32),
            pltpu.SemaphoreType.DMA((4,)),
        ],
        compiler_params=params,
        name="pack",
    )(orbitals, face_metric, cross_metric, screen)
    pieces = packed[:groups]
    far, near, inverse, metric = packed[groups:]

    def swap(x, s):
        return lax.ppermute(x, "orb", [(i, i ^ s) for i in range(groups)])

    to_near = [(i, i ^ 1) for i in range(slabs)]
    to_far = []
    for g in range(groups):
        to_far += [(g * slabs + i, g * slabs + ((i + 1) ^ 1) - 1) for i in range(1, slabs - 1)]
        to_far += [(g * slabs + i, (g ^ 1) * slabs + i) for i in (0, slabs - 1)]
    gathered = [pieces[0]] + [swap(pieces[s], s) for s in range(1, groups)]
    far_side = lax.ppermute(far, ("orb", "dom"), to_far)
    near_side = lax.ppermute(near, "dom", to_near)
    rest = jnp.concatenate(gathered[1:], axis=0)
    far_rest = lax.ppermute(rest, ("orb", "dom"), to_far)
    near_rest = lax.ppermute(rest, "dom", to_near)

    room = sz.turns * sz.orbs + BATCH
    field = pltpu.VMEM((BATCH, sz.span, TALL, lanes), f32)
    shares = pl.pallas_call(
        functools.partial(relax_kernel, sz, slabs),
        out_shape=[jax.ShapeDtypeStruct((mine, planes, sz.rows, lanes), f32)] * groups,
        in_specs=[hbm] + [vmem] * (groups + 6),
        out_specs=[vmem] * groups,
        scratch_shapes=[
            pltpu.VMEM((sz.orbs, sz.span, TALL, lanes), f32),
            pltpu.VMEM((sz.span, TALL, lanes), f32),
            pltpu.VMEM((9, sz.span, 16, lanes), f32),
            field,
            field,
            field,
            pltpu.VMEM((sz.orbs, planes, 8, lanes), f32),
            pltpu.SMEM((room,), jnp.int32),
            pltpu.SMEM((room,), jnp.int32),
            pltpu.SMEM((room,), jnp.int32),
            pltpu.SMEM((sz.orbs,), jnp.int32),
            pltpu.SMEM((sz.orbs,), jnp.int32),
            pltpu.SMEM((sz.turns,), jnp.int32),
            pltpu.SemaphoreType.DMA(()),
        ],
        compiler_params=params,
        name="relax",
    )(turn_orbital, *gathered, far_side, near_side, far_rest, near_rest, inverse, metric)
    blocks = [shares[0]] + [swap(shares[s], s) for s in range(1, groups)]
    return pl.pallas_call(
        functools.partial(unpack_kernel, sz),
        out_shape=jax.ShapeDtypeStruct((mine, planes, height, lanes), f32),
        in_specs=[vmem] * groups,
        out_specs=vmem,
        compiler_params=params,
        name="unpack",
    )(*blocks)


def solution(mesh):
    in_specs = (
        P("orb", "dom", None, None),
        P(None, "dom", None, None),
        P(None, "dom", None, None),
        P("dom", None, None),
        P(),
    )
    out_specs = P("orb", "dom", None, None)
    return jax.shard_map(
        functools.partial(body, mesh.shape["orb"], mesh.shape["dom"]),
        mesh=mesh,
        in_specs=in_specs,
        out_specs=out_specs,
        check_vma=False,
    )
```

```python
import functools

import jax
import jax.numpy as jnp
from jax import lax
from jax.experimental import pallas as pl
from jax.experimental.pallas import tpu as pltpu
from jax.sharding import PartitionSpec as P

SWEEPS = 6
DEEP = SWEEPS - 1
BATCH = 4
WIDTH = 2
LANES = 128
TOP = 7
TALL = 32
LIMIT = 24 * 1024 * 1024


def padded_to_tile(rows):
    return -(-rows // 8) * 8


class Sizes:
    def __init__(self, groups, mine, planes, height, turns):
        self.groups, self.mine, self.planes, self.turns = groups, mine, planes, turns
        self.height = height
        self.orbs = groups * mine
        self.rows = height // groups
        self.window = self.rows + 2 * DEEP
        self.inner = self.window - 2
        self.span = planes + 2 * DEEP
        self.edge = DEEP - 1
        self.orb_rows = mine * planes * self.window
        self.orb_pack = padded_to_tile(self.orb_rows)
        self.metric_at = DEEP * self.window
        self.orb_at = self.metric_at + 6 * self.edge * self.inner
        self.side_pack = padded_to_tile(self.orb_at + self.orb_rows)


def pack_kernel(sz, orb_in, face_in, cross_in, screen_in, *refs):
    pieces = refs[: sz.groups]
    far_ref, near_ref, inv_ref, met_ref, orb_pad, met_pad = refs[sz.groups : sz.groups + 6]
    orb_ref, face_ref, cross_ref, screen_ref, sems = refs[sz.groups + 6 :]
    copies = [
        pltpu.make_async_copy(source, target, sems.at[i])
        for i, (source, target) in enumerate(
            ((orb_in, orb_ref), (face_in, face_ref), (cross_in, cross_ref), (screen_in, screen_ref))
        )
    ]
    for copy in copies:
        copy.start()
    group = lax.axis_index("orb")
    odd = lax.rem(lax.axis_index("dom"), 2)
    zeros = jnp.zeros((8, LANES), jnp.float32)
    end = 8 + sz.height
    for copy in copies:
        copy.wait()
    for p in range(sz.planes):
        for j in range(sz.mine):
            orb_pad[j, p, 0:8] = zeros
            orb_pad[j, p, end : end + 8] = zeros
            orb_pad[j, p, 8:end] = orb_ref[j, p]
        diag = screen_ref[p] + 2.0 * (face_ref[0, p] + face_ref[1, p] + face_ref[2, p])
        diag = diag + (jnp.abs(cross_ref[0, p]) + jnp.abs(cross_ref[1, p]) + jnp.abs(cross_ref[2, p]))
        met_pad[6, p, 8:end] = 1.0 / diag
        for c in range(3):
            met_pad[c, p, 8:end] = face_ref[c, p]
            met_pad[3 + c, p, 8:end] = 0.25 * cross_ref[c, p]
        for c in range(7):
            met_pad[c, p, 0:8] = zeros
            met_pad[c, p, end : end + 8] = zeros
    own = 8 + group * sz.rows - DEEP
    for s in range(sz.groups):
        first = 8 + jnp.bitwise_xor(group, s) * sz.rows - DEEP
        for j in range(sz.mine):
            for p in range(sz.planes):
                at = (j * sz.planes + p) * sz.window
                pieces[s][at : at + sz.window] = orb_pad[j, p, pl.ds(first, sz.window)]
    for ref, from_end in ((far_ref, odd), (near_ref, 1 - odd)):
        first_inv = from_end * (sz.planes - DEEP)
        first_met = from_end * (sz.planes - sz.edge)
        for p in range(DEEP):
            at = p * sz.window
            ref[at : at + sz.window] = met_pad[6, first_inv + p, pl.ds(own, sz.window)]
        for c in range(6):
            for p in range(sz.edge):
                at = sz.metric_at + (c * sz.edge + p) * sz.inner
                ref[at : at + sz.inner] = met_pad[c, first_met + p, pl.ds(own + 1, sz.inner)]
        for j in range(sz.mine):
            for p in range(DEEP):
                at = sz.orb_at + (j * DEEP + p) * sz.window
                ref[at : at + sz.window] = orb_pad[j, first_inv + p, pl.ds(own, sz.window)]
    for p in range(sz.planes):
        inv_ref[p, 0 : sz.window] = met_pad[6, p, pl.ds(own, sz.window)]
        for c in range(6):
            met_ref[c, p, 0 : sz.inner] = met_pad[c, p, pl.ds(own + 1, sz.inner)]


def list_pairs(sz, group, turn_ref, first_ref, second_ref, weight_ref, seen_ref, mult_ref):
    def slot_of(k):
        return jnp.bitwise_xor(k // sz.mine, group) * sz.mine + lax.rem(k, sz.mine)

    for i in range(sz.orbs):
        seen_ref[i] = 0
        mult_ref[i] = 0
    slots = [slot_of(turn_ref[t]) for t in range(sz.turns)]
    for k in slots:
        mult_ref[k] = mult_ref[k] + 1
    count = jnp.int32(0)
    for k in slots:
        fresh = 1 - seen_ref[k]
        times = mult_ref[k]

        def step(i, count, k=k, fresh=fresh, times=times):
            first_ref[count] = k
            second_ref[count] = i
            weight_ref[count] = times + mult_ref[i]
            return count + fresh * (1 - seen_ref[i])

        count = lax.fori_loop(0, sz.orbs, step, count)
        seen_ref[k] = 1
    for i in range(BATCH):
        first_ref[count + i] = 0
        second_ref[count + i] = 0
        weight_ref[count + i] = 0
    return count


def mirrored(odd, p, count):
    return p + odd * (count - 1 - 2 * p)


def start_turns(turn_in, turn_ref, sem):
    turns = pltpu.make_async_copy(turn_in, turn_ref, sem)
    turns.start()
    return turns


def fill_own(sz, odd, gathered, orbs):
    n, win = sz.planes, sz.window
    for p in range(n):
        to = DEEP + mirrored(odd, p, n)
        for s in range(sz.groups):
            for j in range(sz.mine):
                at = (j * n + p) * win
                orbs[s * sz.mine + j, to, TOP : TOP + win] = gathered[s][at : at + win]


def fill_side(sz, odd, base, side, rest, orbs):
    n, win = sz.planes, sz.window
    for p in range(DEEP):
        to = base + mirrored(odd, p, DEEP)
        for j in range(sz.mine):
            row = sz.orb_at + (j * DEEP + p) * win
            orbs[j, to, TOP : TOP + win] = side[row : row + win]
        for i in range(sz.orbs - sz.mine):
            row = (i // sz.mine) * sz.orb_pack + ((i % sz.mine) * n + p) * win
            orbs[sz.mine + i, to, TOP : TOP + win] = rest[row : row + win]


def fill_start(sz, orbs, inv, start, fields, firsts, seconds, planes):
    for p in planes:
        for r, size in ((TOP, 8), (TOP + 8, 8), (TOP + 16, 2)):
            scale = inv[p, r : r + size]
            for f in fields:
                start[f, p, r : r + size] = (
                    orbs[firsts[f], p, r : r + size] * orbs[seconds[f], p, r : r + size] * scale
                )


def sweep(source, start, coef, fields, row, planes, put):
    values = {}

    def fetch(f, p):
        up = source(f, p, row + 1)
        down = source(f, p, row - 1)
        return source(f, p, row), up - down, up + down

    for f in fields:
        values[f, planes[0] - 1] = fetch(f, planes[0] - 1)
        values[f, planes[0]] = fetch(f, planes[0])
    for p in planes:
        cs = [coef[c, p, row - 8 : row] for c in range(9)]
        for f in fields:
            values[f, p + 1] = fetch(f, p + 1)
            before, diff_before, _ = values.pop((f, p - 1))
            here, diff, both = values[f, p]
            after, diff_after, _ = values[f, p + 1]
            slope = after - before
            up = cs[3] * here + cs[4] * slope + cs[5] * diff
            down = cs[6] * here + cs[7] * slope + cs[8] * diff
            new = start[f, p, row : row + 8] + cs[0] * (after + before)
            new = new + cs[1] * both + cs[2] * (diff_after - diff_before)
            new = new + (pltpu.roll(up, LANES - 1, 1) + pltpu.roll(down, 1, 1))
            put(f, p, new)


HALVES = [range(f, f + WIDTH) for f in range(0, BATCH, WIDTH)]


def near_kernel(sz, slabs, turn_in, *refs):
    gathered = refs[: sz.groups]
    far_ref, near_ref, near_rest, inv_ref, met_ref, inv, coef, state = refs[sz.groups : sz.groups + 8]
    orbs, start, *refs = refs[sz.groups + 8 :]
    levels, (first_ref, second_ref, weight_ref, seen_ref, mult_ref, turn_ref, sem) = refs[: DEEP - 2], refs[DEEP - 2 :]
    turns = start_turns(turn_in, turn_ref, sem)
    group = lax.axis_index("orb")
    slab = lax.axis_index("dom")
    odd = lax.rem(slab, 2)
    inside = jnp.where((slab == 0) | (slab == slabs - 1), 0.0, 1.0)
    n, win = sz.planes, sz.window
    above = n + DEEP

    fill_own(sz, odd, gathered, orbs)
    fill_side(sz, odd, above, near_ref, near_rest, orbs)
    for p in range(n):
        to = DEEP + mirrored(odd, p, n)
        inv[to, TOP : TOP + win] = inv_ref[p, 0:win]
        for c in range(6):
            coef[c, to, 0 : sz.inner] = met_ref[c, p, 0 : sz.inner]
    for ref, base, first, live in ((far_ref, 0, 1, inside), (near_ref, above, 0, 1.0)):
        for p in range(DEEP):
            inv[base + mirrored(odd, p, DEEP), TOP : TOP + win] = ref[p * win : (p + 1) * win] * live
        for c in range(6):
            for p in range(sz.edge):
                row = sz.metric_at + (c * sz.edge + p) * sz.inner
                coef[c, base + first + mirrored(odd, p, sz.edge), 0 : sz.inner] = ref[row : row + sz.inner]

    lane = lax.broadcasted_iota(jnp.int32, (8, LANES), 1)
    side = (1 - 2 * odd).astype(jnp.float32)
    for p in range(1, sz.span - 1):
        for r in (0, 8):
            scale = inv[p, 8 + r : 16 + r]
            along = scale * side
            fx, fy, fz, xy, xz, yz = [
                coef[c, p, r : r + 8] * (along if c in (3, 4) else scale) for c in range(6)
            ]
            coef[0, p, r : r + 8] = fx
            coef[1, p, r : r + 8] = fy
            coef[2, p, r : r + 8] = xy
            for at, values, sign in ((3, fz, 1.0), (4, xz, -1.0), (5, yz, -1.0)):
                up = jnp.where(lane == 0, 0.0, pltpu.roll(values, 1, 1))
                down = jnp.where(lane == LANES - 1, 0.0, pltpu.roll(values, LANES - 1, 1))
                coef[at, p, r : r + 8] = up
                coef[at + 3, p, r : r + 8] = sign * down
    turns.wait()
    count = list_pairs(sz, group, turn_ref, first_ref, second_ref, weight_ref, seen_ref, mult_ref)

    def batch(index, carry):
        base = index * BATCH
        firsts = [first_ref[base + f] for f in range(BATCH)]
        seconds = [second_ref[base + f] for f in range(BATCH)]
        for fields in HALVES:
            fill_start(sz, orbs, inv, start, fields, firsts, seconds, range(DEEP, sz.span))
        for number in range(1, DEEP):
            for fields in HALVES:
                source = start if number == 1 else levels[number - 2]
                planes = list(range(DEEP + number, sz.span - number))
                for row in (8, 16):

                    def load(f, p, at, source=source):
                        return source[f, p, at : at + 8]

                    def put(f, p, new, row=row, number=number):
                        if number < DEEP - 1:
                            levels[number - 1][f, p, row : row + 8] = new
                        if p < DEEP + number + 2:
                            state[base + f, number - 1, p - DEEP - number, row : row + 8] = new

                    sweep(load, start, coef, fields, row, planes, put)
        return carry

    lax.fori_loop(0, (count + BATCH - 1) // BATCH, batch, 0)


def far_kernel(sz, turn_in, *refs):
    gathered = refs[: sz.groups]
    far_ref, far_rest, inv, coef, state = refs[sz.groups : sz.groups + 5]
    outs = refs[sz.groups + 5 : 2 * sz.groups + 5]
    orbs, total, start, *refs = refs[2 * sz.groups + 5 :]
    levels, (first_ref, second_ref, weight_ref, seen_ref, mult_ref, turn_ref, sem) = refs[: DEEP - 1], refs[DEEP - 1 :]
    turns = start_turns(turn_in, turn_ref, sem)
    group = lax.axis_index("orb")
    odd = lax.rem(lax.axis_index("dom"), 2)
    n = sz.planes
    fill_own(sz, odd, gathered, orbs)
    fill_side(sz, odd, 0, far_ref, far_rest, orbs)
    for i in range(sz.orbs):
        for p in range(n):
            total[i, p] = jnp.zeros((8, LANES), jnp.float32)
    turns.wait()
    count = list_pairs(sz, group, turn_ref, first_ref, second_ref, weight_ref, seen_ref, mult_ref)

    def batch(index, carry):
        base = index * BATCH
        firsts = [first_ref[base + f] for f in range(BATCH)]
        seconds = [second_ref[base + f] for f in range(BATCH)]
        weights = []
        for f in range(BATCH):
            w = weight_ref[base + f]
            weights.append(
                (w.astype(jnp.float32), jnp.where(firsts[f] == seconds[f], 0, w).astype(jnp.float32))
            )
        for fields in HALVES:
            fill_start(sz, orbs, inv, start, fields, firsts, seconds, range(DEEP + n))
        for number in range(1, DEEP + 1):
            for fields in HALVES:
                planes = list(range(number, number + n))

                def load(f, p, at, number=number):
                    if number == 1:
                        return start[f, p, at : at + 8]
                    if p < number - 1 + n:
                        return levels[number - 2][f, p, at : at + 8]
                    return state[base + f, number - 2, p - (number - 1 + n), at : at + 8]

                if number < DEEP:
                    for row in (8, 16):

                        def put(f, p, new, row=row, number=number):
                            levels[number - 1][f, p, row : row + 8] = new

                        sweep(load, start, coef, fields, row, planes, put)
                else:
                    row = TOP + DEEP

                    def put(f, p, new, row=row):
                        a, b = firsts[f], seconds[f]
                        q = p - DEEP
                        total[a, q] = total[a, q] + (weights[f][0] * new) * orbs[b, p, row : row + 8]
                        total[b, q] = total[b, q] + (weights[f][1] * new) * orbs[a, p, row : row + 8]

                    sweep(load, start, coef, fields, row, planes, put)
        return carry

    lax.fori_loop(0, (count + BATCH - 1) // BATCH, batch, 0)

    for s in range(sz.groups):
        for j in range(sz.mine):
            for p in range(n):
                outs[s][j, p] = total[s * sz.mine + j, mirrored(odd, p, n), 0 : sz.rows]


def unpack_kernel(sz, *refs):
    blocks, out_ref = refs[: sz.groups], refs[sz.groups]
    group = lax.axis_index("orb")
    for s in range(sz.groups):
        first = jnp.bitwise_xor(group, s) * sz.rows
        if sz.rows % 8 == 0:
            first = pl.multiple_of(first, 8)
        for j in range(sz.mine):
            for p in range(sz.planes):
                out_ref[j, p, pl.ds(first, sz.rows)] = blocks[s][j, p]


def body(groups, slabs, orbitals, face_metric, cross_metric, screen, turn_orbital):
    mine, planes, height, lanes = orbitals.shape
    sz = Sizes(groups, mine, planes, height, turn_orbital.shape[0])
    f32 = jnp.float32
    vmem = pl.BlockSpec(memory_space=pltpu.VMEM)
    hbm = pl.BlockSpec(memory_space=pltpu.HBM)
    params = pltpu.CompilerParams(vmem_limit_bytes=LIMIT)

    packed = pl.pallas_call(
        functools.partial(pack_kernel, sz),
        out_shape=[jax.ShapeDtypeStruct((sz.orb_pack, lanes), f32)] * groups
        + [jax.ShapeDtypeStruct((sz.side_pack, lanes), f32)] * 2
        + [
            jax.ShapeDtypeStruct((planes, 24, lanes), f32),
            jax.ShapeDtypeStruct((6, planes, 16, lanes), f32),
        ],
        in_specs=[hbm] * 4,
        out_specs=[vmem] * (groups + 4),
        scratch_shapes=[
            pltpu.VMEM((mine, planes, height + 16, lanes), f32),
            pltpu.VMEM((7, planes, height + 16, lanes), f32),
            pltpu.VMEM((mine, planes, height, lanes), f32),
            pltpu.VMEM((3, planes, height, lanes), f32),
            pltpu.VMEM((3, planes, height, lanes), f32),
            pltpu.VMEM((planes, height, lanes), f32),
            pltpu.SemaphoreType.DMA((4,)),
        ],
        compiler_params=params,
        name="pack",
    )(*[pltpu.with_memory_space_constraint(x, pltpu.HBM) for x in (orbitals, face_metric, cross_metric, screen)])
    pieces = packed[:groups]
    far, near, inverse, metric = packed[groups:]

    def swap(x, s):
        return lax.ppermute(x, "orb", [(i, i ^ s) for i in range(groups)])

    to_near = [(i, i ^ 1) for i in range(slabs)]
    to_far = []
    for g in range(groups):
        to_far += [(g * slabs + i, g * slabs + ((i + 1) ^ 1) - 1) for i in range(1, slabs - 1)]
        to_far += [(g * slabs + i, (g ^ 1) * slabs + i) for i in (0, slabs - 1)]
    gathered = [pieces[0]] + [swap(pieces[s], s) for s in range(1, groups)]
    far_side = lax.ppermute(far, ("orb", "dom"), to_far)
    near_side = lax.ppermute(near, "dom", to_near)
    rest = jnp.concatenate(gathered[1:], axis=0)
    far_rest = lax.ppermute(rest, ("orb", "dom"), to_far)
    near_rest = lax.ppermute(rest, "dom", to_near)

    turns = sz.turns
    most = turns * sz.orbs - turns * (turns - 1) // 2
    most = -(-most // BATCH) * BATCH
    room = turns * sz.orbs + BATCH
    field = pltpu.VMEM((BATCH, sz.span, TALL, lanes), f32)
    orbital_windows = pltpu.VMEM((sz.orbs, sz.span, TALL, lanes), f32)
    lists = [
        pltpu.SMEM((room,), jnp.int32),
        pltpu.SMEM((room,), jnp.int32),
        pltpu.SMEM((room,), jnp.int32),
        pltpu.SMEM((sz.orbs,), jnp.int32),
        pltpu.SMEM((sz.orbs,), jnp.int32),
        pltpu.SMEM((turns,), jnp.int32),
        pltpu.SemaphoreType.DMA(()),
    ]
    which = pltpu.with_memory_space_constraint(turn_orbital, pltpu.HBM)
    points = sz.rows * planes * lanes
    inverse, coefs, state = pl.pallas_call(
        functools.partial(near_kernel, sz, slabs),
        out_shape=[
            jax.ShapeDtypeStruct((sz.span, TALL, lanes), f32),
            jax.ShapeDtypeStruct((9, sz.span, 16, lanes), f32),
            jax.ShapeDtypeStruct((most, DEEP - 1, 2, TALL, lanes), f32),
        ],
        in_specs=[hbm] + [vmem] * (groups + 5),
        out_specs=[vmem] * 3,
        scratch_shapes=[orbital_windows] + [field] * (DEEP - 1) + lists,
        compiler_params=params,
        cost_estimate=pl.CostEstimate(flops=200 * most * points, bytes_accessed=20_000_000, transcendentals=0),
        name="near",
    )(which, *gathered, far_side, near_side, near_rest, inverse, metric)
    shares = pl.pallas_call(
        functools.partial(far_kernel, sz),
        out_shape=[jax.ShapeDtypeStruct((mine, planes, sz.rows, lanes), f32)] * groups,
        in_specs=[hbm] + [vmem] * (groups + 5),
        out_specs=[vmem] * groups,
        scratch_shapes=[orbital_windows, pltpu.VMEM((sz.orbs, planes, 8, lanes), f32)] + [field] * DEEP + lists,
        compiler_params=params,
        name="far",
    )(which, *gathered, far_side, far_rest, inverse, coefs, state)
    blocks = [shares[0]] + [swap(shares[s], s) for s in range(1, groups)]
    return pl.pallas_call(
        functools.partial(unpack_kernel, sz),
        out_shape=jax.ShapeDtypeStruct((mine, planes, height, lanes), f32),
        in_specs=[vmem] * groups,
        out_specs=vmem,
        compiler_params=params,
        name="unpack",
    )(*blocks)


def solution(mesh):
    in_specs = (
        P("orb", "dom", None, None),
        P(None, "dom", None, None),
        P(None, "dom", None, None),
        P("dom", None, None),
        P(),
    )
    out_specs = P("orb", "dom", None, None)
    return jax.shard_map(
        functools.partial(body, mesh.shape["orb"], mesh.shape["dom"]),
        mesh=mesh,
        in_specs=in_specs,
        out_specs=out_specs,
        check_vma=False,
    )
```

```python
import functools

import jax
import jax.numpy as jnp
from jax import lax
from jax.experimental import pallas as pl
from jax.experimental.pallas import tpu as pltpu
from jax.sharding import PartitionSpec as P

SWEEPS = 6
DEEP = SWEEPS - 1
PARTS = (range(0, 2), range(2, 4), range(4, 7))
BATCH = PARTS[-1][-1] + 1
LANES = 128
TOP = 7
TALL = 32
LIMIT = 24 * 1024 * 1024


def padded_to_tile(rows):
    return -(-rows // 8) * 8


class Sizes:
    def __init__(self, groups, mine, planes, height, turns):
        self.groups, self.mine, self.planes, self.turns = groups, mine, planes, turns
        self.height = height
        self.orbs = groups * mine
        self.routes = [0] + sorted(range(1, groups), key=lambda s: (-bin(s).count("1"), s))
        self.rows = height // groups
        self.window = self.rows + 2 * DEEP
        self.inner = self.window - 2
        self.span = planes + 2 * DEEP
        self.edge = DEEP - 1
        self.orb_rows = mine * planes * self.window
        self.orb_pack = padded_to_tile(self.orb_rows)
        self.metric_at = DEEP * self.window
        self.orb_at = self.metric_at + 6 * self.edge * self.inner
        self.side_pack = padded_to_tile(self.orb_at + self.orb_rows)


def pack_kernel(sz, orb_in, face_in, cross_in, screen_in, *refs):
    pieces = refs[: sz.groups]
    far_ref, near_ref, inv_ref, met_ref, orb_pad, met_pad = refs[sz.groups : sz.groups + 6]
    orb_ref, face_ref, cross_ref, screen_ref, sems = refs[sz.groups + 6 :]
    copies = [
        pltpu.make_async_copy(source, target, sems.at[i])
        for i, (source, target) in enumerate(
            ((orb_in, orb_ref), (face_in, face_ref), (cross_in, cross_ref), (screen_in, screen_ref))
        )
    ]
    for copy in copies:
        copy.start()
    group = lax.axis_index("orb")
    odd = lax.rem(lax.axis_index("dom"), 2)
    zeros = jnp.zeros((8, LANES), jnp.float32)
    end = 8 + sz.height
    for copy in copies:
        copy.wait()
    for p in range(sz.planes):
        for j in range(sz.mine):
            orb_pad[j, p, 0:8] = zeros
            orb_pad[j, p, end : end + 8] = zeros
            orb_pad[j, p, 8:end] = orb_ref[j, p]
        diag = screen_ref[p] + 2.0 * (face_ref[0, p] + face_ref[1, p] + face_ref[2, p])
        diag = diag + (jnp.abs(cross_ref[0, p]) + jnp.abs(cross_ref[1, p]) + jnp.abs(cross_ref[2, p]))
        met_pad[6, p, 8:end] = 1.0 / diag
        for c in range(3):
            met_pad[c, p, 8:end] = face_ref[c, p]
            met_pad[3 + c, p, 8:end] = 0.25 * cross_ref[c, p]
        for c in range(7):
            met_pad[c, p, 0:8] = zeros
            met_pad[c, p, end : end + 8] = zeros
    own = 8 + group * sz.rows - DEEP
    for i, s in enumerate(sz.routes):
        first = 8 + jnp.bitwise_xor(group, s) * sz.rows - DEEP
        for j in range(sz.mine):
            for p in range(sz.planes):
                at = (j * sz.planes + p) * sz.window
                pieces[i][at : at + sz.window] = orb_pad[j, p, pl.ds(first, sz.window)]
    for ref, from_end in ((far_ref, odd), (near_ref, 1 - odd)):
        first_inv = from_end * (sz.planes - DEEP)
        first_met = from_end * (sz.planes - sz.edge)
        for p in range(DEEP):
            at = p * sz.window
            ref[at : at + sz.window] = met_pad[6, first_inv + p, pl.ds(own, sz.window)]
        for c in range(6):
            for p in range(sz.edge):
                at = sz.metric_at + (c * sz.edge + p) * sz.inner
                ref[at : at + sz.inner] = met_pad[c, first_met + p, pl.ds(own + 1, sz.inner)]
        for j in range(sz.mine):
            for p in range(DEEP):
                at = sz.orb_at + (j * DEEP + p) * sz.window
                ref[at : at + sz.window] = orb_pad[j, first_inv + p, pl.ds(own, sz.window)]
    for p in range(sz.planes):
        inv_ref[p, 0 : sz.window] = met_pad[6, p, pl.ds(own, sz.window)]
        for c in range(6):
            met_ref[c, p, 0 : sz.inner] = met_pad[c, p, pl.ds(own + 1, sz.inner)]


def list_pairs(sz, group, turn_ref, first_ref, second_ref, weight_ref, seen_ref, mult_ref):
    def slot_of(k):
        return jnp.bitwise_xor(k // sz.mine, group) * sz.mine + lax.rem(k, sz.mine)

    for i in range(sz.orbs):
        seen_ref[i] = 0
        mult_ref[i] = 0
    slots = [slot_of(turn_ref[t]) for t in range(sz.turns)]
    for k in slots:
        mult_ref[k] = mult_ref[k] + 1
    count = jnp.int32(0)
    for k in slots:
        fresh = 1 - seen_ref[k]
        times = mult_ref[k]

        def step(i, count, k=k, fresh=fresh, times=times):
            first_ref[count] = k
            second_ref[count] = i
            weight_ref[count] = times + mult_ref[i]
            return count + fresh * (1 - seen_ref[i])

        count = lax.fori_loop(0, sz.orbs, step, count)
        seen_ref[k] = 1
    for i in range(BATCH):
        first_ref[count + i] = 0
        second_ref[count + i] = 0
        weight_ref[count + i] = 0
    return count


def mirrored(odd, p, count):
    return p + odd * (count - 1 - 2 * p)


def start_turns(turn_in, turn_ref, sem):
    turns = pltpu.make_async_copy(turn_in, turn_ref, sem)
    turns.start()
    return turns


def fill_own(sz, odd, gathered, orbs):
    n, win = sz.planes, sz.window
    for p in range(n):
        to = DEEP + mirrored(odd, p, n)
        for i, s in enumerate(sz.routes):
            for j in range(sz.mine):
                at = (j * n + p) * win
                orbs[s * sz.mine + j, to, TOP : TOP + win] = gathered[i][at : at + win]


def fill_side(sz, odd, base, side, rest, orbs):
    n, win = sz.planes, sz.window
    for p in range(DEEP):
        to = base + mirrored(odd, p, DEEP)
        for j in range(sz.mine):
            row = sz.orb_at + (j * DEEP + p) * win
            orbs[j, to, TOP : TOP + win] = side[row : row + win]
        for i, s in enumerate(sz.routes[1:]):
            for j in range(sz.mine):
                row = i * sz.orb_pack + (j * n + p) * win
                orbs[s * sz.mine + j, to, TOP : TOP + win] = rest[row : row + win]


def fill_start(sz, orbs, inv, start, fields, firsts, seconds, planes):
    for p in planes:
        for r, size in ((TOP, 8), (TOP + 8, 8), (TOP + 16, 2)):
            scale = inv[p, r : r + size]
            for f in fields:
                start[f - fields[0], p, r : r + size] = (
                    orbs[firsts[f], p, r : r + size] * orbs[seconds[f], p, r : r + size] * scale
                )


def sweep(source, start, coef, fields, row, planes, put):
    values = {}

    def fetch(f, p):
        up = source(f, p, row + 1)
        down = source(f, p, row - 1)
        return source(f, p, row), up - down, up + down

    for f in fields:
        values[f, planes[0] - 1] = fetch(f, planes[0] - 1)
        values[f, planes[0]] = fetch(f, planes[0])
    for p in planes:
        cs = [coef[c, p, row - 8 : row] for c in range(9)]
        for f in fields:
            values[f, p + 1] = fetch(f, p + 1)
            before, diff_before, _ = values.pop((f, p - 1))
            here, diff, both = values[f, p]
            after, diff_after, _ = values[f, p + 1]
            slope = after - before
            up = cs[3] * here + cs[4] * slope + cs[5] * diff
            down = cs[6] * here + cs[7] * slope + cs[8] * diff
            new = start[f - fields[0], p, row : row + 8] + cs[0] * (after + before)
            new = new + cs[1] * both + cs[2] * (diff_after - diff_before)
            put(f, p, new + (pltpu.roll(up, LANES - 1, 1) + pltpu.roll(down, 1, 1)))


def near_kernel(sz, slabs, turn_in, *refs):
    gathered = refs[: sz.groups]
    far_ref, near_ref, near_rest, inv_ref, met_ref, inv, coef, state = refs[sz.groups : sz.groups + 8]
    orbs, *refs = refs[sz.groups + 8 :]
    starts, refs = refs[: len(PARTS)], refs[len(PARTS) :]
    every = len(PARTS) * (DEEP - 2)
    levels, (first_ref, second_ref, weight_ref, seen_ref, mult_ref, turn_ref, sem) = refs[:every], refs[every:]
    turns = start_turns(turn_in, turn_ref, sem)
    group = lax.axis_index("orb")
    slab = lax.axis_index("dom")
    odd = lax.rem(slab, 2)
    inside = jnp.where((slab == 0) | (slab == slabs - 1), 0.0, 1.0)
    n, win = sz.planes, sz.window
    above = n + DEEP

    fill_own(sz, odd, gathered, orbs)
    fill_side(sz, odd, above, near_ref, near_rest, orbs)
    for p in range(n):
        to = DEEP + mirrored(odd, p, n)
        inv[to, TOP : TOP + win] = inv_ref[p, 0:win]
        for c in range(6):
            coef[c, to, 0 : sz.inner] = met_ref[c, p, 0 : sz.inner]
    for ref, base, first, live in ((far_ref, 0, 1, inside), (near_ref, above, 0, 1.0)):
        for p in range(DEEP):
            inv[base + mirrored(odd, p, DEEP), TOP : TOP + win] = ref[p * win : (p + 1) * win] * live
        for c in range(6):
            for p in range(sz.edge):
                row = sz.metric_at + (c * sz.edge + p) * sz.inner
                coef[c, base + first + mirrored(odd, p, sz.edge), 0 : sz.inner] = ref[row : row + sz.inner]

    lane = lax.broadcasted_iota(jnp.int32, (8, LANES), 1)
    side = (1 - 2 * odd).astype(jnp.float32)
    for p in range(1, sz.span - 1):
        for r in (0, 8):
            scale = inv[p, 8 + r : 16 + r]
            along = scale * side
            fx, fy, fz, xy, xz, yz = [
                coef[c, p, r : r + 8] * (along if c in (3, 4) else scale) for c in range(6)
            ]
            coef[0, p, r : r + 8] = fx
            coef[1, p, r : r + 8] = fy
            coef[2, p, r : r + 8] = xy
            for at, values, sign in ((3, fz, 1.0), (4, xz, -1.0), (5, yz, -1.0)):
                up = jnp.where(lane == 0, 0.0, pltpu.roll(values, 1, 1))
                down = jnp.where(lane == LANES - 1, 0.0, pltpu.roll(values, LANES - 1, 1))
                coef[at, p, r : r + 8] = up
                coef[at + 3, p, r : r + 8] = sign * down
    turns.wait()
    count = list_pairs(sz, group, turn_ref, first_ref, second_ref, weight_ref, seen_ref, mult_ref)

    def batch(index, carry):
        base = index * BATCH
        firsts = [first_ref[base + f] for f in range(BATCH)]
        seconds = [second_ref[base + f] for f in range(BATCH)]
        for fields, start in zip(PARTS, starts):
            fill_start(sz, orbs, inv, start, fields, firsts, seconds, range(DEEP, sz.span))
        for number in range(1, DEEP):
            for h, fields in enumerate(PARTS):
                start, low = starts[h], fields[0]
                source = start if number == 1 else levels[h * (DEEP - 2) + number - 2]
                planes = list(range(DEEP + number, sz.span - number))
                for row in (8, 16):

                    def load(f, p, at, source=source, low=low):
                        return source[f - low, p, at : at + 8]

                    def put(f, p, new, row=row, number=number, low=low, h=h):
                        if number < DEEP - 1:
                            levels[h * (DEEP - 2) + number - 1][f - low, p, row : row + 8] = new
                        if p < DEEP + number + 2:
                            state[base + f, number - 1, p - DEEP - number, row : row + 8] = new

                    sweep(load, start, coef, fields, row, planes, put)
        return carry

    lax.fori_loop(0, (count + BATCH - 1) // BATCH, batch, 0)


def far_kernel(sz, turn_in, *refs):
    gathered = refs[: sz.groups]
    far_ref, far_rest, inv, coef, state = refs[sz.groups : sz.groups + 5]
    outs = refs[sz.groups + 5 : 2 * sz.groups + 5]
    orbs, total, *refs = refs[2 * sz.groups + 5 :]
    starts, refs = refs[: len(PARTS)], refs[len(PARTS) :]
    every = len(PARTS) * (DEEP - 1)
    levels, (first_ref, second_ref, weight_ref, seen_ref, mult_ref, turn_ref, sem) = refs[:every], refs[every:]
    turns = start_turns(turn_in, turn_ref, sem)
    group = lax.axis_index("orb")
    odd = lax.rem(lax.axis_index("dom"), 2)
    n = sz.planes
    fill_own(sz, odd, gathered, orbs)
    fill_side(sz, odd, 0, far_ref, far_rest, orbs)
    for i in range(sz.orbs):
        for p in range(n):
            total[i, p] = jnp.zeros((8, LANES), jnp.float32)
    turns.wait()
    count = list_pairs(sz, group, turn_ref, first_ref, second_ref, weight_ref, seen_ref, mult_ref)

    def batch(index, carry):
        base = index * BATCH
        firsts = [first_ref[base + f] for f in range(BATCH)]
        seconds = [second_ref[base + f] for f in range(BATCH)]
        weights = []
        for f in range(BATCH):
            w = weight_ref[base + f]
            weights.append(
                (w.astype(jnp.float32), jnp.where(firsts[f] == seconds[f], 0, w).astype(jnp.float32))
            )
        for fields, start in zip(PARTS, starts):
            fill_start(sz, orbs, inv, start, fields, firsts, seconds, range(DEEP + n))
        for number in range(1, DEEP + 1):
            for h, fields in enumerate(PARTS):
                start, low = starts[h], fields[0]
                planes = list(range(number, number + n))

                def load(f, p, at, number=number, start=start, low=low, h=h):
                    if number == 1:
                        return start[f - low, p, at : at + 8]
                    if p < number - 1 + n:
                        return levels[h * (DEEP - 1) + number - 2][f - low, p, at : at + 8]
                    return state[base + f, number - 2, p - (number - 1 + n), at : at + 8]

                if number < DEEP:
                    for row in (8, 16):

                        def put(f, p, new, row=row, number=number, low=low, h=h):
                            levels[h * (DEEP - 1) + number - 1][f - low, p, row : row + 8] = new

                        sweep(load, start, coef, fields, row, planes, put)
                else:
                    row = TOP + DEEP

                    def put(f, p, new, row=row):
                        a, b = firsts[f], seconds[f]
                        q = p - DEEP
                        total[a, q] = total[a, q] + (weights[f][0] * new) * orbs[b, p, row : row + 8]
                        total[b, q] = total[b, q] + (weights[f][1] * new) * orbs[a, p, row : row + 8]

                    sweep(load, start, coef, fields, row, planes, put)
        return carry

    lax.fori_loop(0, (count + BATCH - 1) // BATCH, batch, 0)

    for i, s in enumerate(sz.routes):
        for j in range(sz.mine):
            for p in range(n):
                outs[i][j, p] = total[s * sz.mine + j, mirrored(odd, p, n), 0 : sz.rows]


def unpack_kernel(sz, *refs):
    blocks, out_ref = refs[: sz.groups], refs[sz.groups]
    group = lax.axis_index("orb")
    for i, s in enumerate(sz.routes):
        first = jnp.bitwise_xor(group, s) * sz.rows
        if sz.rows % 8 == 0:
            first = pl.multiple_of(first, 8)
        for j in range(sz.mine):
            for p in range(sz.planes):
                out_ref[j, p, pl.ds(first, sz.rows)] = blocks[i][j, p]


def body(groups, slabs, orbitals, face_metric, cross_metric, screen, turn_orbital):
    mine, planes, height, lanes = orbitals.shape
    sz = Sizes(groups, mine, planes, height, turn_orbital.shape[0])
    f32 = jnp.float32
    vmem = pl.BlockSpec(memory_space=pltpu.VMEM)
    hbm = pl.BlockSpec(memory_space=pltpu.HBM)
    params = pltpu.CompilerParams(vmem_limit_bytes=LIMIT)

    packed = pl.pallas_call(
        functools.partial(pack_kernel, sz),
        out_shape=[jax.ShapeDtypeStruct((sz.orb_pack, lanes), f32)] * groups
        + [jax.ShapeDtypeStruct((sz.side_pack, lanes), f32)] * 2
        + [
            jax.ShapeDtypeStruct((planes, 24, lanes), f32),
            jax.ShapeDtypeStruct((6, planes, 16, lanes), f32),
        ],
        in_specs=[hbm] * 4,
        out_specs=[vmem] * (groups + 4),
        scratch_shapes=[
            pltpu.VMEM((mine, planes, height + 16, lanes), f32),
            pltpu.VMEM((7, planes, height + 16, lanes), f32),
            pltpu.VMEM((mine, planes, height, lanes), f32),
            pltpu.VMEM((3, planes, height, lanes), f32),
            pltpu.VMEM((3, planes, height, lanes), f32),
            pltpu.VMEM((planes, height, lanes), f32),
            pltpu.SemaphoreType.DMA((4,)),
        ],
        compiler_params=params,
        name="pack",
    )(*[pltpu.with_memory_space_constraint(x, pltpu.HBM) for x in (orbitals, face_metric, cross_metric, screen)])
    pieces = packed[:groups]
    far, near, inverse, metric = packed[groups:]

    def swap(x, s):
        return lax.ppermute(x, "orb", [(i, i ^ s) for i in range(groups)])

    to_near = [(i, i ^ 1) for i in range(slabs)]
    to_far = []
    for g in range(groups):
        to_far += [(g * slabs + i, g * slabs + ((i + 1) ^ 1) - 1) for i in range(1, slabs - 1)]
        to_far += [(g * slabs + i, (g ^ 1) * slabs + i) for i in (0, slabs - 1)]
    gathered = [pieces[0]] + [swap(piece, s) for piece, s in zip(pieces[1:], sz.routes[1:])]
    far_side = lax.ppermute(far, ("orb", "dom"), to_far)
    near_side = lax.ppermute(near, "dom", to_near)
    rest = jnp.concatenate(gathered[1:], axis=0)
    far_rest = lax.ppermute(rest, ("orb", "dom"), to_far)
    near_rest = lax.ppermute(rest, "dom", to_near)

    turns = sz.turns
    most = turns * sz.orbs - turns * (turns - 1) // 2
    most = -(-most // BATCH) * BATCH
    room = turns * sz.orbs + BATCH
    field = [pltpu.VMEM((len(fields), sz.span, TALL, lanes), f32) for fields in PARTS]
    orbital_windows = pltpu.VMEM((sz.orbs, sz.span, TALL, lanes), f32)
    lists = [
        pltpu.SMEM((room,), jnp.int32),
        pltpu.SMEM((room,), jnp.int32),
        pltpu.SMEM((room,), jnp.int32),
        pltpu.SMEM((sz.orbs,), jnp.int32),
        pltpu.SMEM((sz.orbs,), jnp.int32),
        pltpu.SMEM((turns,), jnp.int32),
        pltpu.SemaphoreType.DMA(()),
    ]
    which = pltpu.with_memory_space_constraint(turn_orbital, pltpu.HBM)
    points = sz.rows * planes * lanes
    inverse, coefs, state = pl.pallas_call(
        functools.partial(near_kernel, sz, slabs),
        out_shape=[
            jax.ShapeDtypeStruct((sz.span, TALL, lanes), f32),
            jax.ShapeDtypeStruct((9, sz.span, 16, lanes), f32),
            jax.ShapeDtypeStruct((most, DEEP - 1, 2, TALL, lanes), f32),
        ],
        in_specs=[hbm] + [vmem] * (groups + 5),
        out_specs=[vmem] * 3,
        scratch_shapes=[orbital_windows] + field + [x for x in field for _ in range(DEEP - 2)] + lists,
        compiler_params=params,
        cost_estimate=pl.CostEstimate(flops=200 * most * points, bytes_accessed=20_000_000, transcendentals=0),
        name="near",
    )(which, *gathered, far_side, near_side, near_rest, inverse, metric)
    shares = pl.pallas_call(
        functools.partial(far_kernel, sz),
        out_shape=[jax.ShapeDtypeStruct((mine, planes, sz.rows, lanes), f32)] * groups,
        in_specs=[hbm] + [vmem] * (groups + 5),
        out_specs=[vmem] * groups,
        scratch_shapes=[orbital_windows, pltpu.VMEM((sz.orbs, planes, 8, lanes), f32)]
        + field
        + [x for x in field for _ in range(DEEP - 1)]
        + lists,
        compiler_params=params,
        name="far",
    )(which, *gathered, far_side, far_rest, inverse, coefs, state)
    blocks = [shares[0]] + [swap(share, s) for share, s in zip(shares[1:], sz.routes[1:])]
    return pl.pallas_call(
        functools.partial(unpack_kernel, sz),
        out_shape=jax.ShapeDtypeStruct((mine, planes, height, lanes), f32),
        in_specs=[vmem] * groups,
        out_specs=vmem,
        compiler_params=params,
        name="unpack",
    )(*blocks)


def solution(mesh):
    in_specs = (
        P("orb", "dom", None, None),
        P(None, "dom", None, None),
        P(None, "dom", None, None),
        P("dom", None, None),
        P(),
    )
    out_specs = P("orb", "dom", None, None)
    return jax.shard_map(
        functools.partial(body, mesh.shape["orb"], mesh.shape["dom"]),
        mesh=mesh,
        in_specs=in_specs,
        out_specs=out_specs,
        check_vma=False,
    )
```

```python
import functools

import jax
import jax.numpy as jnp
from jax import lax
from jax.experimental import pallas as pl
from jax.experimental.pallas import tpu as pltpu
from jax.sharding import PartitionSpec as P

SWEEPS = 6
DEEP = SWEEPS - 1
PARTS = (range(0, 2), range(2, 4), range(4, 7))
BATCH = PARTS[-1][-1] + 1
LANES = 128
TOP = 7
TALL = 32
LIMIT = 24 * 1024 * 1024


def padded_to_tile(rows):
    return -(-rows // 8) * 8


class Sizes:
    def __init__(self, groups, mine, planes, height, turns):
        self.groups, self.mine, self.planes, self.turns = groups, mine, planes, turns
        self.height = height
        self.orbs = groups * mine
        self.routes = [0] + sorted(range(1, groups), key=lambda s: (-bin(s).count("1"), s))
        self.rows = height // groups
        self.window = self.rows + 2 * DEEP
        self.inner = self.window - 2
        self.span = planes + 2 * DEEP
        self.edge = DEEP - 1
        self.orb_rows = mine * planes * self.window
        self.orb_pack = padded_to_tile(self.orb_rows)
        self.metric_at = DEEP * self.window
        self.orb_at = self.metric_at + 6 * self.edge * self.inner
        self.side_pack = padded_to_tile(self.orb_at + self.orb_rows)


def pack_kernel(sz, orb_in, face_in, cross_in, screen_in, *refs):
    pieces = refs[: sz.groups]
    far_ref, near_ref, inv_ref, met_ref, orb_pad, met_pad = refs[sz.groups : sz.groups + 6]
    orb_ref, face_ref, cross_ref, screen_ref, sems = refs[sz.groups + 6 :]
    copies = [
        pltpu.make_async_copy(source, target, sems.at[i])
        for i, (source, target) in enumerate(
            ((orb_in, orb_ref), (face_in, face_ref), (cross_in, cross_ref), (screen_in, screen_ref))
        )
    ]
    for copy in copies:
        copy.start()
    group = lax.axis_index("orb")
    odd = lax.rem(lax.axis_index("dom"), 2)
    zeros = jnp.zeros((8, LANES), jnp.float32)
    end = 8 + sz.height
    for copy in copies:
        copy.wait()
    for p in range(sz.planes):
        for j in range(sz.mine):
            orb_pad[j, p, 0:8] = zeros
            orb_pad[j, p, end : end + 8] = zeros
            orb_pad[j, p, 8:end] = orb_ref[j, p]
        diag = screen_ref[p] + 2.0 * (face_ref[0, p] + face_ref[1, p] + face_ref[2, p])
        diag = diag + (jnp.abs(cross_ref[0, p]) + jnp.abs(cross_ref[1, p]) + jnp.abs(cross_ref[2, p]))
        met_pad[6, p, 8:end] = 1.0 / diag
        for c in range(3):
            met_pad[c, p, 8:end] = face_ref[c, p]
            met_pad[3 + c, p, 8:end] = 0.25 * cross_ref[c, p]
        for c in range(7):
            met_pad[c, p, 0:8] = zeros
            met_pad[c, p, end : end + 8] = zeros
    own = 8 + group * sz.rows - DEEP
    for i, s in enumerate(sz.routes):
        first = 8 + jnp.bitwise_xor(group, s) * sz.rows - DEEP
        for j in range(sz.mine):
            for p in range(sz.planes):
                at = (j * sz.planes + p) * sz.window
                pieces[i][at : at + sz.window] = orb_pad[j, p, pl.ds(first, sz.window)]
    for ref, from_end in ((far_ref, odd), (near_ref, 1 - odd)):
        first_inv = from_end * (sz.planes - DEEP)
        first_met = from_end * (sz.planes - sz.edge)
        for p in range(DEEP):
            at = p * sz.window
            ref[at : at + sz.window] = met_pad[6, first_inv + p, pl.ds(own, sz.window)]
        for c in range(6):
            for p in range(sz.edge):
                at = sz.metric_at + (c * sz.edge + p) * sz.inner
                ref[at : at + sz.inner] = met_pad[c, first_met + p, pl.ds(own + 1, sz.inner)]
        for j in range(sz.mine):
            for p in range(DEEP):
                at = sz.orb_at + (j * DEEP + p) * sz.window
                ref[at : at + sz.window] = orb_pad[j, first_inv + p, pl.ds(own, sz.window)]
    for p in range(sz.planes):
        inv_ref[p, 0 : sz.window] = met_pad[6, p, pl.ds(own, sz.window)]
        for c in range(6):
            met_ref[c, p, 0 : sz.inner] = met_pad[c, p, pl.ds(own + 1, sz.inner)]


def list_kernel(sz, turn_in, list_ref, seen_ref, mult_ref, turn_ref, sem):
    turns = pltpu.make_async_copy(turn_in, turn_ref, sem)
    turns.start()
    group = lax.axis_index("orb")

    def slot_of(k):
        return jnp.bitwise_xor(k // sz.mine, group) * sz.mine + lax.rem(k, sz.mine)

    for i in range(sz.orbs):
        seen_ref[i] = 0
        mult_ref[i] = 0
    turns.wait()
    slots = [slot_of(turn_ref[t]) for t in range(sz.turns)]
    for k in slots:
        mult_ref[k] = mult_ref[k] + 1
    count = jnp.int32(0)

    def write(count, first, second, weight):
        at = 1 + 3 * count
        list_ref[at] = first
        list_ref[at + 1] = second
        list_ref[at + 2] = weight

    for k in slots:
        fresh = 1 - seen_ref[k]
        times = mult_ref[k]

        def step(i, count, k=k, fresh=fresh, times=times):
            write(count, k, i, times + mult_ref[i])
            return count + fresh * (1 - seen_ref[i])

        count = lax.fori_loop(0, sz.orbs, step, count)
        seen_ref[k] = 1
    for i in range(BATCH):
        write(count + i, 0, 0, 0)
    list_ref[0] = (count + BATCH - 1) // BATCH


def mirrored(odd, p, count):
    return p + odd * (count - 1 - 2 * p)


def fill_own(sz, odd, gathered, orbs):
    n, win = sz.planes, sz.window
    for p in range(n):
        to = DEEP + mirrored(odd, p, n)
        for i, s in enumerate(sz.routes):
            for j in range(sz.mine):
                at = (j * n + p) * win
                orbs[s * sz.mine + j, to, TOP : TOP + win] = gathered[i][at : at + win]


def fill_side(sz, odd, base, side, rest, orbs):
    n, win = sz.planes, sz.window
    for p in range(DEEP):
        to = base + mirrored(odd, p, DEEP)
        for j in range(sz.mine):
            row = sz.orb_at + (j * DEEP + p) * win
            orbs[j, to, TOP : TOP + win] = side[row : row + win]
        for i, s in enumerate(sz.routes[1:]):
            for j in range(sz.mine):
                row = i * sz.orb_pack + (j * n + p) * win
                orbs[s * sz.mine + j, to, TOP : TOP + win] = rest[row : row + win]


def fill_start(sz, orbs, inv, start, fields, firsts, seconds, planes):
    for p in planes:
        for r, size in ((TOP, 8), (TOP + 8, 8), (TOP + 16, 2)):
            scale = inv[p, r : r + size]
            for f in fields:
                start[f - fields[0], p, r : r + size] = (
                    orbs[firsts[f], p, r : r + size] * orbs[seconds[f], p, r : r + size] * scale
                )


def sweep(source, start, coef, fields, row, planes, put):
    values = {}

    def fetch(f, p):
        up = source(f, p, row + 1)
        down = source(f, p, row - 1)
        return source(f, p, row), up - down, up + down

    for f in fields:
        values[f, planes[0] - 1] = fetch(f, planes[0] - 1)
        values[f, planes[0]] = fetch(f, planes[0])
    for p in planes:
        cs = [coef[c, p, row - 8 : row] for c in range(9)]
        for f in fields:
            values[f, p + 1] = fetch(f, p + 1)
            before, diff_before, _ = values.pop((f, p - 1))
            here, diff, both = values[f, p]
            after, diff_after, _ = values[f, p + 1]
            slope = after - before
            up = cs[3] * here + cs[4] * slope + cs[5] * diff
            down = cs[6] * here + cs[7] * slope + cs[8] * diff
            new = start[f - fields[0], p, row : row + 8] + cs[0] * (after + before)
            new = new + cs[1] * both + cs[2] * (diff_after - diff_before)
            put(f, p, new + (pltpu.roll(up, LANES - 1, 1) + pltpu.roll(down, 1, 1)))


def prepare(odd, inv, coef, planes):
    lane = lax.broadcasted_iota(jnp.int32, (8, LANES), 1)
    side = (1 - 2 * odd).astype(jnp.float32)
    for p in planes:
        for r in (0, 8):
            scale = inv[p, 8 + r : 16 + r]
            along = scale * side
            fx, fy, fz, xy, xz, yz = [
                coef[c, p, r : r + 8] * (along if c in (3, 4) else scale) for c in range(6)
            ]
            coef[0, p, r : r + 8] = fx
            coef[1, p, r : r + 8] = fy
            coef[2, p, r : r + 8] = xy
            for at, values, sign in ((3, fz, 1.0), (4, xz, -1.0), (5, yz, -1.0)):
                up = jnp.where(lane == 0, 0.0, pltpu.roll(values, 1, 1))
                down = jnp.where(lane == LANES - 1, 0.0, pltpu.roll(values, LANES - 1, 1))
                coef[at, p, r : r + 8] = up
                coef[at + 3, p, r : r + 8] = sign * down


def take_side(sz, odd, ref, base, first, inv, coef):
    win = sz.window
    for p in range(DEEP):
        inv[base + mirrored(odd, p, DEEP), TOP : TOP + win] = ref[p * win : (p + 1) * win]
    for c in range(6):
        for p in range(sz.edge):
            row = sz.metric_at + (c * sz.edge + p) * sz.inner
            coef[c, base + first + mirrored(odd, p, sz.edge), 0 : sz.inner] = ref[row : row + sz.inner]


def coefs_kernel(sz, near_ref, inv_ref, met_ref, inv, coef):
    odd = lax.rem(lax.axis_index("dom"), 2)
    n = sz.planes
    for p in range(n):
        to = mirrored(odd, p, n)
        inv[to, TOP : TOP + sz.window] = inv_ref[p, 0 : sz.window]
        for c in range(6):
            coef[c, to, 0 : sz.inner] = met_ref[c, p, 0 : sz.inner]
    take_side(sz, odd, near_ref, n, 0, inv, coef)
    prepare(odd, inv, coef, range(n + sz.edge))


class Planes:
    def __init__(self, halo, others):
        self.halo, self.others = halo, others

    def __getitem__(self, at):
        *lead, p, rows = at
        ref, p = (self.halo, p) if p < DEEP else (self.others, p - DEEP)
        return ref[(*lead, p, rows)]


def near_kernel(sz, list_ref, *refs):
    gathered = refs[: sz.groups]
    near_ref, near_rest, inv, coef, state = refs[sz.groups : sz.groups + 5]
    orbs, *refs = refs[sz.groups + 5 :]
    starts, refs = refs[: len(PARTS)], refs[len(PARTS) :]
    every = len(PARTS) * (DEEP - 2)
    levels = refs[:every]
    group = lax.axis_index("orb")
    odd = lax.rem(lax.axis_index("dom"), 2)
    inv, coef = Planes(None, inv), Planes(None, coef)
    fill_own(sz, odd, gathered, orbs)
    fill_side(sz, odd, sz.planes + DEEP, near_ref, near_rest, orbs)

    def batch(index, carry):
        base = index * BATCH
        firsts = [list_ref[1 + 3 * (base + f)] for f in range(BATCH)]
        seconds = [list_ref[2 + 3 * (base + f)] for f in range(BATCH)]
        for fields, start in zip(PARTS, starts):
            fill_start(sz, orbs, inv, start, fields, firsts, seconds, range(DEEP, sz.span))
        for number in range(1, DEEP):
            for h, fields in enumerate(PARTS):
                start, low = starts[h], fields[0]
                source = start if number == 1 else levels[h * (DEEP - 2) + number - 2]
                planes = list(range(DEEP + number, sz.span - number))
                for row in (8, 16):

                    def load(f, p, at, source=source, low=low):
                        return source[f - low, p, at : at + 8]

                    def put(f, p, new, row=row, number=number, low=low, h=h):
                        if number < DEEP - 1:
                            levels[h * (DEEP - 2) + number - 1][f - low, p, row : row + 8] = new
                        if p < DEEP + number + 2:
                            state[base + f, number - 1, p - DEEP - number, row : row + 8] = new

                    sweep(load, start, coef, fields, row, planes, put)
        return carry

    lax.fori_loop(0, list_ref[0], batch, 0)


def far_kernel(sz, slabs, list_ref, *refs):
    gathered = refs[: sz.groups]
    far_ref, far_rest, inv, coef, state = refs[sz.groups : sz.groups + 5]
    outs = refs[sz.groups + 5 : 2 * sz.groups + 5]
    orbs, total, inv_far, coef_far, *refs = refs[2 * sz.groups + 5 :]
    starts, refs = refs[: len(PARTS)], refs[len(PARTS) :]
    every = len(PARTS) * (DEEP - 1)
    levels = refs[:every]
    group = lax.axis_index("orb")
    slab = lax.axis_index("dom")
    odd = lax.rem(slab, 2)
    n = sz.planes
    take_side(sz, odd, far_ref, 0, 1, inv_far, coef_far)
    inside = jnp.where((slab == 0) | (slab == slabs - 1), 0.0, 1.0)
    for p in range(DEEP):
        inv_far[p, 0:TALL] = inv_far[p, 0:TALL] * inside
    prepare(odd, inv_far, coef_far, range(1, DEEP))
    inv, coef = Planes(inv_far, inv), Planes(coef_far, coef)
    fill_own(sz, odd, gathered, orbs)
    fill_side(sz, odd, 0, far_ref, far_rest, orbs)
    for i in range(sz.orbs):
        for p in range(n):
            total[i, p] = jnp.zeros((8, LANES), jnp.float32)

    def batch(index, carry):
        base = index * BATCH
        firsts = [list_ref[1 + 3 * (base + f)] for f in range(BATCH)]
        seconds = [list_ref[2 + 3 * (base + f)] for f in range(BATCH)]
        weights = []
        for f in range(BATCH):
            w = list_ref[3 + 3 * (base + f)]
            weights.append(
                (w.astype(jnp.float32), jnp.where(firsts[f] == seconds[f], 0, w).astype(jnp.float32))
            )
        for fields, start in zip(PARTS, starts):
            fill_start(sz, orbs, inv, start, fields, firsts, seconds, range(DEEP + n))
        for number in range(1, DEEP + 1):
            for h, fields in enumerate(PARTS):
                start, low = starts[h], fields[0]
                planes = list(range(number, number + n))

                def load(f, p, at, number=number, start=start, low=low, h=h):
                    if number == 1:
                        return start[f - low, p, at : at + 8]
                    if p < number - 1 + n:
                        return levels[h * (DEEP - 1) + number - 2][f - low, p, at : at + 8]
                    return state[base + f, number - 2, p - (number - 1 + n), at : at + 8]

                if number < DEEP:
                    for row in (8, 16):

                        def put(f, p, new, row=row, number=number, low=low, h=h):
                            levels[h * (DEEP - 1) + number - 1][f - low, p, row : row + 8] = new

                        sweep(load, start, coef, fields, row, planes, put)
                else:
                    row = TOP + DEEP

                    def put(f, p, new, row=row):
                        a, b = firsts[f], seconds[f]
                        q = p - DEEP
                        total[a, q] = total[a, q] + (weights[f][0] * new) * orbs[b, p, row : row + 8]
                        total[b, q] = total[b, q] + (weights[f][1] * new) * orbs[a, p, row : row + 8]

                    sweep(load, start, coef, fields, row, planes, put)
        return carry

    lax.fori_loop(0, list_ref[0], batch, 0)

    for i, s in enumerate(sz.routes):
        for j in range(sz.mine):
            for p in range(n):
                outs[i][j, p] = total[s * sz.mine + j, mirrored(odd, p, n), 0 : sz.rows]


def unpack_kernel(sz, *refs):
    blocks, out_ref = refs[: sz.groups], refs[sz.groups]
    group = lax.axis_index("orb")
    for i, s in enumerate(sz.routes):
        first = jnp.bitwise_xor(group, s) * sz.rows
        if sz.rows % 8 == 0:
            first = pl.multiple_of(first, 8)
        for j in range(sz.mine):
            for p in range(sz.planes):
                out_ref[j, p, pl.ds(first, sz.rows)] = blocks[i][j, p]


def body(groups, slabs, orbitals, face_metric, cross_metric, screen, turn_orbital):
    mine, planes, height, lanes = orbitals.shape
    sz = Sizes(groups, mine, planes, height, turn_orbital.shape[0])
    f32 = jnp.float32
    vmem = pl.BlockSpec(memory_space=pltpu.VMEM)
    hbm = pl.BlockSpec(memory_space=pltpu.HBM)
    smem = pl.BlockSpec(memory_space=pltpu.SMEM)
    params = pltpu.CompilerParams(vmem_limit_bytes=LIMIT)

    packed = pl.pallas_call(
        functools.partial(pack_kernel, sz),
        out_shape=[jax.ShapeDtypeStruct((sz.orb_pack, lanes), f32)] * groups
        + [jax.ShapeDtypeStruct((sz.side_pack, lanes), f32)] * 2
        + [
            jax.ShapeDtypeStruct((planes, 24, lanes), f32),
            jax.ShapeDtypeStruct((6, planes, 16, lanes), f32),
        ],
        in_specs=[hbm] * 4,
        out_specs=[vmem] * (groups + 4),
        scratch_shapes=[
            pltpu.VMEM((mine, planes, height + 16, lanes), f32),
            pltpu.VMEM((7, planes, height + 16, lanes), f32),
            pltpu.VMEM((mine, planes, height, lanes), f32),
            pltpu.VMEM((3, planes, height, lanes), f32),
            pltpu.VMEM((3, planes, height, lanes), f32),
            pltpu.VMEM((planes, height, lanes), f32),
            pltpu.SemaphoreType.DMA((4,)),
        ],
        compiler_params=params,
        name="pack",
    )(*[pltpu.with_memory_space_constraint(x, pltpu.HBM) for x in (orbitals, face_metric, cross_metric, screen)])
    pieces = packed[:groups]
    far, near, inverse, metric = packed[groups:]

    def swap(x, s):
        return lax.ppermute(x, "orb", [(i, i ^ s) for i in range(groups)])

    to_near = [(i, i ^ 1) for i in range(slabs)]
    to_far = []
    for g in range(groups):
        to_far += [(g * slabs + i, g * slabs + ((i + 1) ^ 1) - 1) for i in range(1, slabs - 1)]
        to_far += [(g * slabs + i, (g ^ 1) * slabs + i) for i in (0, slabs - 1)]
    gathered = [pieces[0]] + [swap(piece, s) for piece, s in zip(pieces[1:], sz.routes[1:])]
    far_side = lax.ppermute(far, ("orb", "dom"), to_far)
    near_side = lax.ppermute(near, "dom", to_near)
    turns = sz.turns
    most = turns * sz.orbs - turns * (turns - 1) // 2
    most = -(-most // BATCH) * BATCH
    room = turns * sz.orbs + BATCH
    which = pltpu.with_memory_space_constraint(turn_orbital, pltpu.HBM)
    points = sz.rows * planes * lanes
    pairs = pl.pallas_call(
        functools.partial(list_kernel, sz),
        out_shape=jax.ShapeDtypeStruct((1 + 3 * room,), jnp.int32),
        in_specs=[hbm],
        out_specs=smem,
        scratch_shapes=[
            pltpu.SMEM((sz.orbs,), jnp.int32),
            pltpu.SMEM((sz.orbs,), jnp.int32),
            pltpu.SMEM((turns,), jnp.int32),
            pltpu.SemaphoreType.DMA(()),
        ],
        compiler_params=params,
        name="pairs",
    )(which)
    inverse, coefs = pl.pallas_call(
        functools.partial(coefs_kernel, sz),
        out_shape=[
            jax.ShapeDtypeStruct((planes + DEEP, TALL, lanes), f32),
            jax.ShapeDtypeStruct((9, planes + DEEP, 16, lanes), f32),
        ],
        in_specs=[vmem] * 3,
        out_specs=[vmem] * 2,
        compiler_params=params,
        cost_estimate=pl.CostEstimate(flops=50 * points, bytes_accessed=2_500_000, transcendentals=0),
        name="coefs",
    )(near_side, inverse, metric)
    *gathered, pairs, inverse, coefs = lax.optimization_barrier((*gathered, pairs, inverse, coefs))
    rest = jnp.concatenate(gathered[1:], axis=0)
    far_rest = lax.ppermute(rest, ("orb", "dom"), to_far)
    near_rest = lax.ppermute(rest, "dom", to_near)

    field = [pltpu.VMEM((len(fields), sz.span, TALL, lanes), f32) for fields in PARTS]
    orbital_windows = pltpu.VMEM((sz.orbs, sz.span, TALL, lanes), f32)
    state = pl.pallas_call(
        functools.partial(near_kernel, sz),
        out_shape=jax.ShapeDtypeStruct((most, DEEP - 1, 2, TALL, lanes), f32),
        in_specs=[smem] + [vmem] * (groups + 4),
        out_specs=vmem,
        scratch_shapes=[orbital_windows] + field + [x for x in field for _ in range(DEEP - 2)],
        compiler_params=params,
        cost_estimate=pl.CostEstimate(flops=200 * most * points, bytes_accessed=20_000_000, transcendentals=0),
        name="near",
    )(pairs, *gathered, near_side, near_rest, inverse, coefs)
    shares = pl.pallas_call(
        functools.partial(far_kernel, sz, slabs),
        out_shape=[jax.ShapeDtypeStruct((mine, planes, sz.rows, lanes), f32)] * groups,
        in_specs=[smem] + [vmem] * (groups + 5),
        out_specs=[vmem] * groups,
        scratch_shapes=[
            orbital_windows,
            pltpu.VMEM((sz.orbs, planes, 8, lanes), f32),
            pltpu.VMEM((DEEP, TALL, lanes), f32),
            pltpu.VMEM((9, DEEP, 16, lanes), f32),
        ]
        + field
        + [x for x in field for _ in range(DEEP - 1)]
       ,
        compiler_params=params,
        name="far",
    )(pairs, *gathered, far_side, far_rest, inverse, coefs, state)
    blocks = [shares[0]] + [swap(share, s) for share, s in zip(shares[1:], sz.routes[1:])]
    return pl.pallas_call(
        functools.partial(unpack_kernel, sz),
        out_shape=jax.ShapeDtypeStruct((mine, planes, height, lanes), f32),
        in_specs=[vmem] * groups,
        out_specs=vmem,
        compiler_params=params,
        name="unpack",
    )(*blocks)


def solution(mesh):
    in_specs = (
        P("orb", "dom", None, None),
        P(None, "dom", None, None),
        P(None, "dom", None, None),
        P("dom", None, None),
        P(),
    )
    out_specs = P("orb", "dom", None, None)
    return jax.shard_map(
        functools.partial(body, mesh.shape["orb"], mesh.shape["dom"]),
        mesh=mesh,
        in_specs=in_specs,
        out_specs=out_specs,
        check_vma=False,
    )
```

```python
import functools

import jax
import jax.numpy as jnp
from jax import lax
from jax.experimental import pallas as pl
from jax.experimental.pallas import tpu as pltpu
from jax.sharding import PartitionSpec as P

SWEEPS = 6
DEEP = SWEEPS - 1
FULL = ((0, range(0, 2)), (1, range(2, 4)), (2, range(4, 7)))
SHORT = ((0, range(0, 2)), (2, range(2, 5)))
PARTS = [fields for _, fields in FULL]
BATCH, REST = FULL[-1][1][-1] + 1, SHORT[-1][1][-1] + 1
LANES = 128
TOP = 7
TALL = 32
LIMIT = 24 * 1024 * 1024


def padded_to_tile(rows):
    return -(-rows // 8) * 8


class Sizes:
    def __init__(self, groups, mine, planes, height, turns):
        self.groups, self.mine, self.planes, self.turns = groups, mine, planes, turns
        self.height = height
        self.orbs = groups * mine
        self.routes = [0] + sorted(range(1, groups), key=lambda s: (-bin(s).count("1"), s))
        self.rows = height // groups
        self.window = self.rows + 2 * DEEP
        self.inner = self.window - 2
        self.span = planes + 2 * DEEP
        self.edge = DEEP - 1
        self.orb_rows = mine * planes * self.window
        self.orb_pack = padded_to_tile(self.orb_rows)
        self.metric_at = DEEP * self.window
        self.orb_at = self.metric_at + 6 * self.edge * self.inner
        self.side_pack = padded_to_tile(self.orb_at + self.orb_rows)


def pack_kernel(sz, orb_in, face_in, cross_in, screen_in, *refs):
    pieces = refs[: sz.groups]
    far_ref, near_ref, inv_ref, met_ref, orb_pad, met_pad = refs[sz.groups : sz.groups + 6]
    orb_ref, face_ref, cross_ref, screen_ref, sems = refs[sz.groups + 6 :]
    copies = [
        pltpu.make_async_copy(source, target, sems.at[i])
        for i, (source, target) in enumerate(
            ((orb_in, orb_ref), (face_in, face_ref), (cross_in, cross_ref), (screen_in, screen_ref))
        )
    ]
    for copy in copies:
        copy.start()
    group = lax.axis_index("orb")
    odd = lax.rem(lax.axis_index("dom"), 2)
    zeros = jnp.zeros((8, LANES), jnp.float32)
    end = 8 + sz.height
    for p in range(sz.planes):
        for pad in [orb_pad.at[j] for j in range(sz.mine)] + [met_pad.at[c] for c in range(7)]:
            pad[p, 0:8] = zeros
            pad[p, end : end + 8] = zeros
    copies[0].wait()
    for p in range(sz.planes):
        for j in range(sz.mine):
            orb_pad[j, p, 8:end] = orb_ref[j, p]
    own = 8 + group * sz.rows - DEEP
    for i, s in enumerate(sz.routes):
        first = 8 + jnp.bitwise_xor(group, s) * sz.rows - DEEP
        for j in range(sz.mine):
            for p in range(sz.planes):
                at = (j * sz.planes + p) * sz.window
                pieces[i][at : at + sz.window] = orb_pad[j, p, pl.ds(first, sz.window)]
    for copy in copies[1:]:
        copy.wait()
    for p in range(sz.planes):
        diag = screen_ref[p] + 2.0 * (face_ref[0, p] + face_ref[1, p] + face_ref[2, p])
        diag = diag + (jnp.abs(cross_ref[0, p]) + jnp.abs(cross_ref[1, p]) + jnp.abs(cross_ref[2, p]))
        met_pad[6, p, 8:end] = 1.0 / diag
        for c in range(3):
            met_pad[c, p, 8:end] = face_ref[c, p]
            met_pad[3 + c, p, 8:end] = 0.25 * cross_ref[c, p]
    for ref, from_end in ((far_ref, odd), (near_ref, 1 - odd)):
        first_inv = from_end * (sz.planes - DEEP)
        first_met = from_end * (sz.planes - sz.edge)
        for p in range(DEEP):
            at = p * sz.window
            ref[at : at + sz.window] = met_pad[6, first_inv + p, pl.ds(own, sz.window)]
        for c in range(6):
            for p in range(sz.edge):
                at = sz.metric_at + (c * sz.edge + p) * sz.inner
                ref[at : at + sz.inner] = met_pad[c, first_met + p, pl.ds(own + 1, sz.inner)]
        for j in range(sz.mine):
            for p in range(DEEP):
                at = sz.orb_at + (j * DEEP + p) * sz.window
                ref[at : at + sz.window] = orb_pad[j, first_inv + p, pl.ds(own, sz.window)]
    for p in range(sz.planes):
        inv_ref[p, 0 : sz.window] = met_pad[6, p, pl.ds(own, sz.window)]
        for c in range(6):
            met_ref[c, p, 0 : sz.inner] = met_pad[c, p, pl.ds(own + 1, sz.inner)]


def list_kernel(sz, turn_in, list_ref, seen_ref, mult_ref, turn_ref, sem):
    turns = pltpu.make_async_copy(turn_in, turn_ref, sem)
    turns.start()
    group = lax.axis_index("orb")

    def slot_of(k):
        return jnp.bitwise_xor(k // sz.mine, group) * sz.mine + lax.rem(k, sz.mine)

    for i in range(sz.orbs):
        seen_ref[i] = 0
        mult_ref[i] = 0
    turns.wait()
    slots = [slot_of(turn_ref[t]) for t in range(sz.turns)]
    for k in slots:
        mult_ref[k] = mult_ref[k] + 1
    count = jnp.int32(0)

    def write(count, first, second, weight):
        at = 2 + 3 * count
        list_ref[at] = first
        list_ref[at + 1] = second
        list_ref[at + 2] = weight

    for k in slots:
        fresh = 1 - seen_ref[k]
        times = mult_ref[k]

        def step(i, count, k=k, fresh=fresh, times=times):
            write(count, k, i, times + mult_ref[i])
            return count + fresh * (1 - seen_ref[i])

        count = lax.fori_loop(0, sz.orbs, step, count)
        seen_ref[k] = 1
    for i in range(BATCH):
        write(count + i, 0, 0, 0)
    full = (count + BATCH - 1 - REST) // BATCH
    list_ref[0] = full
    list_ref[1] = jnp.where(full * BATCH < count, 1, 0)


def mirrored(odd, p, count):
    return p + odd * (count - 1 - 2 * p)


def fill_own(sz, odd, gathered, orbs):
    n, win = sz.planes, sz.window
    for p in range(n):
        to = DEEP + mirrored(odd, p, n)
        for i, s in enumerate(sz.routes):
            for j in range(sz.mine):
                at = (j * n + p) * win
                orbs[s * sz.mine + j, to, TOP : TOP + win] = gathered[i][at : at + win]


def fill_side(sz, odd, base, side, rest, orbs):
    n, win = sz.planes, sz.window
    for p in range(DEEP):
        to = base + mirrored(odd, p, DEEP)
        for j in range(sz.mine):
            row = sz.orb_at + (j * DEEP + p) * win
            orbs[j, to, TOP : TOP + win] = side[row : row + win]
        for i, s in enumerate(sz.routes[1:]):
            for j in range(sz.mine):
                row = i * sz.orb_pack + (j * n + p) * win
                orbs[s * sz.mine + j, to, TOP : TOP + win] = rest[row : row + win]


def fill_start(sz, orbs, inv, start, fields, firsts, seconds, planes):
    for p in planes:
        for r, size in ((TOP, 8), (TOP + 8, 8), (TOP + 16, 2)):
            scale = inv[p, r : r + size]
            for f in fields:
                start[f - fields[0], p, r : r + size] = (
                    orbs[firsts[f], p, r : r + size] * orbs[seconds[f], p, r : r + size] * scale
                )


def sweep(source, start, coef, fields, row, planes, put):
    values = {}

    def fetch(f, p):
        up = source(f, p, row + 1)
        down = source(f, p, row - 1)
        return source(f, p, row), up - down, up + down

    for f in fields:
        values[f, planes[0] - 1] = fetch(f, planes[0] - 1)
        values[f, planes[0]] = fetch(f, planes[0])
    for p in planes:
        cs = [coef[c, p, row - 8 : row] for c in range(9)]
        for f in fields:
            values[f, p + 1] = fetch(f, p + 1)
            before, diff_before, _ = values.pop((f, p - 1))
            here, diff, both = values[f, p]
            after, diff_after, _ = values[f, p + 1]
            slope = after - before
            up = cs[3] * here + cs[4] * slope + cs[5] * diff
            down = cs[6] * here + cs[7] * slope + cs[8] * diff
            new = start[f - fields[0], p, row : row + 8] + cs[0] * (after + before)
            new = new + cs[1] * both + cs[2] * (diff_after - diff_before)
            put(f, p, new + (pltpu.roll(up, LANES - 1, 1) + pltpu.roll(down, 1, 1)))


def prepare(odd, inv, coef, planes):
    lane = lax.broadcasted_iota(jnp.int32, (8, LANES), 1)
    side = (1 - 2 * odd).astype(jnp.float32)
    for p in planes:
        for r in (0, 8):
            scale = inv[p, 8 + r : 16 + r]
            along = scale * side
            fx, fy, fz, xy, xz, yz = [
                coef[c, p, r : r + 8] * (along if c in (3, 4) else scale) for c in range(6)
            ]
            coef[0, p, r : r + 8] = fx
            coef[1, p, r : r + 8] = fy
            coef[2, p, r : r + 8] = xy
            for at, values, sign in ((3, fz, 1.0), (4, xz, -1.0), (5, yz, -1.0)):
                up = jnp.where(lane == 0, 0.0, pltpu.roll(values, 1, 1))
                down = jnp.where(lane == LANES - 1, 0.0, pltpu.roll(values, LANES - 1, 1))
                coef[at, p, r : r + 8] = up
                coef[at + 3, p, r : r + 8] = sign * down


def take_side(sz, odd, ref, base, first, inv, coef):
    win = sz.window
    for p in range(DEEP):
        inv[base + mirrored(odd, p, DEEP), TOP : TOP + win] = ref[p * win : (p + 1) * win]
    for c in range(6):
        for p in range(sz.edge):
            row = sz.metric_at + (c * sz.edge + p) * sz.inner
            coef[c, base + first + mirrored(odd, p, sz.edge), 0 : sz.inner] = ref[row : row + sz.inner]


def coefs_kernel(sz, near_ref, inv_ref, met_ref, inv, coef):
    odd = lax.rem(lax.axis_index("dom"), 2)
    n = sz.planes
    for p in range(n):
        to = mirrored(odd, p, n)
        inv[to, TOP : TOP + sz.window] = inv_ref[p, 0 : sz.window]
        for c in range(6):
            coef[c, to, 0 : sz.inner] = met_ref[c, p, 0 : sz.inner]
    take_side(sz, odd, near_ref, n, 0, inv, coef)
    prepare(odd, inv, coef, range(n + sz.edge))


class Planes:
    def __init__(self, halo, others):
        self.halo, self.others = halo, others

    def __getitem__(self, at):
        *lead, p, rows = at
        ref, p = (self.halo, p) if p < DEEP else (self.others, p - DEEP)
        return ref[(*lead, p, rows)]


def near_kernel(sz, list_ref, *refs):
    gathered = refs[: sz.groups]
    near_ref, near_rest, inv, coef, state = refs[sz.groups : sz.groups + 5]
    orbs, *refs = refs[sz.groups + 5 :]
    starts, refs = refs[: len(PARTS)], refs[len(PARTS) :]
    every = len(PARTS) * (DEEP - 2)
    levels = refs[:every]
    group = lax.axis_index("orb")
    odd = lax.rem(lax.axis_index("dom"), 2)
    inv, coef = Planes(None, inv), Planes(None, coef)
    fill_own(sz, odd, gathered, orbs)
    fill_side(sz, odd, sz.planes + DEEP, near_ref, near_rest, orbs)

    def batch(parts, base, carry):
        size = parts[-1][1][-1] + 1
        firsts = [list_ref[2 + 3 * (base + f)] for f in range(size)]
        seconds = [list_ref[3 + 3 * (base + f)] for f in range(size)]
        for h, fields in parts:
            fill_start(sz, orbs, inv, starts[h], fields, firsts, seconds, range(DEEP, sz.span))
        for number in range(1, DEEP):
            for h, fields in parts:
                start, low = starts[h], fields[0]
                source = start if number == 1 else levels[h * (DEEP - 2) + number - 2]
                planes = list(range(DEEP + number, sz.span - number))
                for row in (8, 16):

                    def load(f, p, at, source=source, low=low):
                        return source[f - low, p, at : at + 8]

                    def put(f, p, new, row=row, number=number, low=low, h=h):
                        if number < DEEP - 1:
                            levels[h * (DEEP - 2) + number - 1][f - low, p, row : row + 8] = new
                        if p < DEEP + number + 2:
                            state[base + f, number - 1, p - DEEP - number, row : row + 8] = new

                    sweep(load, start, coef, fields, row, planes, put)
        return carry

    full = list_ref[0]
    lax.fori_loop(0, full, lambda i, carry: batch(FULL, i * BATCH, carry), 0)
    lax.fori_loop(0, list_ref[1], lambda i, carry: batch(SHORT, full * BATCH, carry), 0)


def far_kernel(sz, slabs, list_ref, *refs):
    gathered = refs[: sz.groups]
    far_ref, far_rest, inv, coef, state = refs[sz.groups : sz.groups + 5]
    outs = refs[sz.groups + 5 : 2 * sz.groups + 5]
    orbs, total, inv_far, coef_far, *refs = refs[2 * sz.groups + 5 :]
    starts, refs = refs[: len(PARTS)], refs[len(PARTS) :]
    every = len(PARTS) * (DEEP - 1)
    levels = refs[:every]
    group = lax.axis_index("orb")
    slab = lax.axis_index("dom")
    odd = lax.rem(slab, 2)
    n = sz.planes
    take_side(sz, odd, far_ref, 0, 1, inv_far, coef_far)
    inside = jnp.where((slab == 0) | (slab == slabs - 1), 0.0, 1.0)
    for p in range(DEEP):
        inv_far[p, 0:TALL] = inv_far[p, 0:TALL] * inside
    prepare(odd, inv_far, coef_far, range(1, DEEP))
    inv, coef = Planes(inv_far, inv), Planes(coef_far, coef)
    fill_own(sz, odd, gathered, orbs)
    fill_side(sz, odd, 0, far_ref, far_rest, orbs)
    for i in range(sz.orbs):
        for p in range(n):
            total[i, p] = jnp.zeros((8, LANES), jnp.float32)

    def batch(parts, base, carry):
        size = parts[-1][1][-1] + 1
        firsts = [list_ref[2 + 3 * (base + f)] for f in range(size)]
        seconds = [list_ref[3 + 3 * (base + f)] for f in range(size)]
        weights = []
        for f in range(size):
            w = list_ref[4 + 3 * (base + f)]
            weights.append(
                (w.astype(jnp.float32), jnp.where(firsts[f] == seconds[f], 0, w).astype(jnp.float32))
            )
        for h, fields in parts:
            fill_start(sz, orbs, inv, starts[h], fields, firsts, seconds, range(DEEP + n))
        for number in range(1, DEEP + 1):
            for h, fields in parts:
                start, low = starts[h], fields[0]
                planes = list(range(number, number + n))

                def load(f, p, at, number=number, start=start, low=low, h=h):
                    if number == 1:
                        return start[f - low, p, at : at + 8]
                    if p < number - 1 + n:
                        return levels[h * (DEEP - 1) + number - 2][f - low, p, at : at + 8]
                    return state[base + f, number - 2, p - (number - 1 + n), at : at + 8]

                if number < DEEP:
                    for row in (8, 16):

                        def put(f, p, new, row=row, number=number, low=low, h=h):
                            levels[h * (DEEP - 1) + number - 1][f - low, p, row : row + 8] = new

                        sweep(load, start, coef, fields, row, planes, put)
                else:
                    row = TOP + DEEP

                    def put(f, p, new, row=row):
                        a, b = firsts[f], seconds[f]
                        q = p - DEEP
                        total[a, q] = total[a, q] + (weights[f][0] * new) * orbs[b, p, row : row + 8]
                        total[b, q] = total[b, q] + (weights[f][1] * new) * orbs[a, p, row : row + 8]

                    sweep(load, start, coef, fields, row, planes, put)
        return carry

    full = list_ref[0]
    lax.fori_loop(0, full, lambda i, carry: batch(FULL, i * BATCH, carry), 0)
    lax.fori_loop(0, list_ref[1], lambda i, carry: batch(SHORT, full * BATCH, carry), 0)

    for i, s in enumerate(sz.routes):
        for j in range(sz.mine):
            for p in range(n):
                outs[i][j, p] = total[s * sz.mine + j, mirrored(odd, p, n), 0 : sz.rows]


def unpack_kernel(sz, *refs):
    blocks, out_ref = refs[: sz.groups], refs[sz.groups]
    group = lax.axis_index("orb")
    for i, s in enumerate(sz.routes):
        first = jnp.bitwise_xor(group, s) * sz.rows
        if sz.rows % 8 == 0:
            first = pl.multiple_of(first, 8)
        for j in range(sz.mine):
            for p in range(sz.planes):
                out_ref[j, p, pl.ds(first, sz.rows)] = blocks[i][j, p]


def body(groups, slabs, orbitals, face_metric, cross_metric, screen, turn_orbital):
    mine, planes, height, lanes = orbitals.shape
    sz = Sizes(groups, mine, planes, height, turn_orbital.shape[0])
    f32 = jnp.float32
    vmem = pl.BlockSpec(memory_space=pltpu.VMEM)
    hbm = pl.BlockSpec(memory_space=pltpu.HBM)
    smem = pl.BlockSpec(memory_space=pltpu.SMEM)
    params = pltpu.CompilerParams(vmem_limit_bytes=LIMIT)

    packed = pl.pallas_call(
        functools.partial(pack_kernel, sz),
        out_shape=[jax.ShapeDtypeStruct((sz.orb_pack, lanes), f32)] * groups
        + [jax.ShapeDtypeStruct((sz.side_pack, lanes), f32)] * 2
        + [
            jax.ShapeDtypeStruct((planes, 24, lanes), f32),
            jax.ShapeDtypeStruct((6, planes, 16, lanes), f32),
        ],
        in_specs=[hbm] * 4,
        out_specs=[vmem] * (groups + 4),
        scratch_shapes=[
            pltpu.VMEM((mine, planes, height + 16, lanes), f32),
            pltpu.VMEM((7, planes, height + 16, lanes), f32),
            pltpu.VMEM((mine, planes, height, lanes), f32),
            pltpu.VMEM((3, planes, height, lanes), f32),
            pltpu.VMEM((3, planes, height, lanes), f32),
            pltpu.VMEM((planes, height, lanes), f32),
            pltpu.SemaphoreType.DMA((4,)),
        ],
        compiler_params=params,
        name="pack",
    )(*[pltpu.with_memory_space_constraint(x, pltpu.HBM) for x in (orbitals, face_metric, cross_metric, screen)])
    pieces = packed[:groups]
    far, near, inverse, metric = packed[groups:]

    def swap(x, s):
        return lax.ppermute(x, "orb", [(i, i ^ s) for i in range(groups)])

    to_near = [(i, i ^ 1) for i in range(slabs)]
    to_far = []
    for g in range(groups):
        to_far += [(g * slabs + i, g * slabs + ((i + 1) ^ 1) - 1) for i in range(1, slabs - 1)]
        to_far += [(g * slabs + i, (g ^ 1) * slabs + i) for i in (0, slabs - 1)]
    gathered = [pieces[0]] + [swap(piece, s) for piece, s in zip(pieces[1:], sz.routes[1:])]
    far_side = lax.ppermute(far, ("orb", "dom"), to_far)
    near_side = lax.ppermute(near, "dom", to_near)
    turns = sz.turns
    most = turns * sz.orbs - turns * (turns - 1) // 2
    most = -(-most // BATCH) * BATCH
    room = turns * sz.orbs + BATCH
    which = pltpu.with_memory_space_constraint(turn_orbital, pltpu.HBM)
    points = sz.rows * planes * lanes
    pairs = pl.pallas_call(
        functools.partial(list_kernel, sz),
        out_shape=jax.ShapeDtypeStruct((2 + 3 * room,), jnp.int32),
        in_specs=[hbm],
        out_specs=smem,
        scratch_shapes=[
            pltpu.SMEM((sz.orbs,), jnp.int32),
            pltpu.SMEM((sz.orbs,), jnp.int32),
            pltpu.SMEM((turns,), jnp.int32),
            pltpu.SemaphoreType.DMA(()),
        ],
        compiler_params=params,
        name="pairs",
    )(which)
    inverse, coefs = pl.pallas_call(
        functools.partial(coefs_kernel, sz),
        out_shape=[
            jax.ShapeDtypeStruct((planes + DEEP, TALL, lanes), f32),
            jax.ShapeDtypeStruct((9, planes + DEEP, 16, lanes), f32),
        ],
        in_specs=[vmem] * 3,
        out_specs=[vmem] * 2,
        compiler_params=params,
        cost_estimate=pl.CostEstimate(flops=50 * points, bytes_accessed=2_500_000, transcendentals=0),
        name="coefs",
    )(near_side, inverse, metric)
    *gathered, pairs, inverse, coefs = lax.optimization_barrier((*gathered, pairs, inverse, coefs))
    rest = jnp.concatenate(gathered[1:], axis=0)
    far_rest = lax.ppermute(rest, ("orb", "dom"), to_far)
    near_rest = lax.ppermute(rest, "dom", to_near)

    field = [pltpu.VMEM((len(fields), sz.span, TALL, lanes), f32) for fields in PARTS]
    orbital_windows = pltpu.VMEM((sz.orbs, sz.span, TALL, lanes), f32)
    state = pl.pallas_call(
        functools.partial(near_kernel, sz),
        out_shape=jax.ShapeDtypeStruct((most, DEEP - 1, 2, TALL, lanes), f32),
        in_specs=[smem] + [vmem] * (groups + 4),
        out_specs=vmem,
        scratch_shapes=[orbital_windows] + field + [x for x in field for _ in range(DEEP - 2)],
        compiler_params=params,
        cost_estimate=pl.CostEstimate(flops=200 * most * points, bytes_accessed=20_000_000, transcendentals=0),
        name="near",
    )(pairs, *gathered, near_side, near_rest, inverse, coefs)
    shares = pl.pallas_call(
        functools.partial(far_kernel, sz, slabs),
        out_shape=[jax.ShapeDtypeStruct((mine, planes, sz.rows, lanes), f32)] * groups,
        in_specs=[smem] + [vmem] * (groups + 5),
        out_specs=[vmem] * groups,
        scratch_shapes=[
            orbital_windows,
            pltpu.VMEM((sz.orbs, planes, 8, lanes), f32),
            pltpu.VMEM((DEEP, TALL, lanes), f32),
            pltpu.VMEM((9, DEEP, 16, lanes), f32),
        ]
        + field
        + [x for x in field for _ in range(DEEP - 1)]
       ,
        compiler_params=params,
        name="far",
    )(pairs, *gathered, far_side, far_rest, inverse, coefs, state)
    blocks = [shares[0]] + [swap(share, s) for share, s in zip(shares[1:], sz.routes[1:])]
    return pl.pallas_call(
        functools.partial(unpack_kernel, sz),
        out_shape=jax.ShapeDtypeStruct((mine, planes, height, lanes), f32),
        in_specs=[vmem] * groups,
        out_specs=vmem,
        compiler_params=params,
        name="unpack",
    )(*blocks)


def solution(mesh):
    in_specs = (
        P("orb", "dom", None, None),
        P(None, "dom", None, None),
        P(None, "dom", None, None),
        P("dom", None, None),
        P(),
    )
    out_specs = P("orb", "dom", None, None)
    return jax.shard_map(
        functools.partial(body, mesh.shape["orb"], mesh.shape["dom"]),
        mesh=mesh,
        in_specs=in_specs,
        out_specs=out_specs,
        check_vma=False,
    )
```

```python
import functools

import jax
import jax.numpy as jnp
from jax import lax
from jax.experimental import pallas as pl
from jax.experimental.pallas import tpu as pltpu
from jax.sharding import PartitionSpec as P

SWEEPS = 6
DEEP = SWEEPS - 1
FULL = ((0, range(0, 2)), (1, range(2, 4)), (2, range(4, 7)))
SHORT = ((0, range(0, 2)), (2, range(2, 5)))
PARTS = [fields for _, fields in FULL]
BATCH, REST = FULL[-1][1][-1] + 1, SHORT[-1][1][-1] + 1
LANES = 128
TOP = 7
TALL = 32
LIMIT = 24 * 1024 * 1024


def padded_to_tile(rows):
    return -(-rows // 8) * 8


class Sizes:
    def __init__(self, groups, mine, planes, height, turns):
        self.groups, self.mine, self.planes, self.turns = groups, mine, planes, turns
        self.height = height
        self.orbs = groups * mine
        self.routes = [0] + sorted(range(1, groups), key=lambda s: (-bin(s).count("1"), s))
        self.rows = height // groups
        self.window = self.rows + 2 * DEEP
        self.inner = self.window - 2
        self.span = planes + 2 * DEEP
        self.edge = DEEP - 1
        self.orb_rows = mine * planes * self.window
        self.orb_pack = padded_to_tile(self.orb_rows)
        self.metric_at = DEEP * self.window
        self.orb_at = self.metric_at + 6 * self.edge * self.inner
        self.side_pack = padded_to_tile(self.orb_at + self.orb_rows)


def pack_kernel(sz, orb_in, face_in, cross_in, screen_in, *refs):
    pieces = refs[: sz.groups]
    far_ref, near_ref, inv_ref, met_ref, orb_pad, met_pad = refs[sz.groups : sz.groups + 6]
    orb_ref, face_ref, cross_ref, screen_ref, sems = refs[sz.groups + 6 :]
    copies = [
        pltpu.make_async_copy(source, target, sems.at[i])
        for i, (source, target) in enumerate(
            ((orb_in, orb_ref), (face_in, face_ref), (cross_in, cross_ref), (screen_in, screen_ref))
        )
    ]
    for copy in copies:
        copy.start()
    group = lax.axis_index("orb")
    odd = lax.rem(lax.axis_index("dom"), 2)
    zeros = jnp.zeros((8, LANES), jnp.float32)
    end = 8 + sz.height
    for p in range(sz.planes):
        for pad in [orb_pad.at[j] for j in range(sz.mine)] + [met_pad.at[c] for c in range(7)]:
            pad[p, 0:8] = zeros
            pad[p, end : end + 8] = zeros
    copies[0].wait()
    for p in range(sz.planes):
        for j in range(sz.mine):
            orb_pad[j, p, 8:end] = orb_ref[j, p]
    own = 8 + group * sz.rows - DEEP
    for i, s in enumerate(sz.routes):
        first = 8 + jnp.bitwise_xor(group, s) * sz.rows - DEEP
        for j in range(sz.mine):
            for p in range(sz.planes):
                at = (j * sz.planes + p) * sz.window
                pieces[i][at : at + sz.window] = orb_pad[j, p, pl.ds(first, sz.window)]
    for copy in copies[1:]:
        copy.wait()
    for p in range(sz.planes):
        diag = screen_ref[p] + 2.0 * (face_ref[0, p] + face_ref[1, p] + face_ref[2, p])
        diag = diag + (jnp.abs(cross_ref[0, p]) + jnp.abs(cross_ref[1, p]) + jnp.abs(cross_ref[2, p]))
        met_pad[6, p, 8:end] = 1.0 / diag
        for c in range(3):
            met_pad[c, p, 8:end] = face_ref[c, p]
            met_pad[3 + c, p, 8:end] = 0.25 * cross_ref[c, p]
    for ref, from_end in ((far_ref, odd), (near_ref, 1 - odd)):
        first_inv = from_end * (sz.planes - DEEP)
        first_met = from_end * (sz.planes - sz.edge)
        for p in range(DEEP):
            at = p * sz.window
            ref[at : at + sz.window] = met_pad[6, first_inv + p, pl.ds(own, sz.window)]
        for c in range(6):
            for p in range(sz.edge):
                at = sz.metric_at + (c * sz.edge + p) * sz.inner
                ref[at : at + sz.inner] = met_pad[c, first_met + p, pl.ds(own + 1, sz.inner)]
        for j in range(sz.mine):
            for p in range(DEEP):
                at = sz.orb_at + (j * DEEP + p) * sz.window
                ref[at : at + sz.window] = orb_pad[j, first_inv + p, pl.ds(own, sz.window)]
    for p in range(sz.planes):
        inv_ref[p, 0 : sz.window] = met_pad[6, p, pl.ds(own, sz.window)]
        for c in range(6):
            met_ref[c, p, 0 : sz.inner] = met_pad[c, p, pl.ds(own + 1, sz.inner)]


def list_kernel(sz, turn_in, list_ref, seen_ref, mult_ref, turn_ref, sem):
    turns = pltpu.make_async_copy(turn_in, turn_ref, sem)
    turns.start()
    group = lax.axis_index("orb")

    def slot_of(k):
        return jnp.bitwise_xor(k // sz.mine, group) * sz.mine + lax.rem(k, sz.mine)

    for i in range(sz.orbs):
        seen_ref[i] = 0
        mult_ref[i] = 0
    turns.wait()
    slots = [slot_of(turn_ref[t]) for t in range(sz.turns)]
    for k in slots:
        mult_ref[k] = mult_ref[k] + 1
    count = jnp.int32(0)

    def write(count, first, second, weight):
        at = 2 + 3 * count
        list_ref[at] = first
        list_ref[at + 1] = second
        list_ref[at + 2] = weight

    for k in slots:
        fresh = 1 - seen_ref[k]
        times = mult_ref[k]

        def step(i, count, k=k, fresh=fresh, times=times):
            write(count, k, i, times + mult_ref[i])
            return count + fresh * (1 - seen_ref[i])

        count = lax.fori_loop(0, sz.orbs, step, count)
        seen_ref[k] = 1
    for i in range(BATCH):
        write(count + i, 0, 0, 0)
    full = (count + BATCH - 1 - REST) // BATCH
    list_ref[0] = full
    list_ref[1] = jnp.where(full * BATCH < count, 1, 0)


def mirrored(odd, p, count):
    return p + odd * (count - 1 - 2 * p)


def fill_own(sz, odd, gathered, orbs):
    n, win = sz.planes, sz.window
    for p in range(n):
        to = DEEP + mirrored(odd, p, n)
        for i, s in enumerate(sz.routes):
            for j in range(sz.mine):
                at = (j * n + p) * win
                orbs[s * sz.mine + j, to, TOP : TOP + win] = gathered[i][at : at + win]


def fill_side(sz, odd, base, side, rest, orbs):
    n, win = sz.planes, sz.window
    for p in range(DEEP):
        to = base + mirrored(odd, p, DEEP)
        for j in range(sz.mine):
            row = sz.orb_at + (j * DEEP + p) * win
            orbs[j, to, TOP : TOP + win] = side[row : row + win]
        for i, s in enumerate(sz.routes[1:]):
            for j in range(sz.mine):
                row = i * sz.orb_pack + (j * n + p) * win
                orbs[s * sz.mine + j, to, TOP : TOP + win] = rest[row : row + win]


def fill_start(sz, orbs, inv, start, fields, firsts, seconds, planes):
    for p in planes:
        for r, size in ((TOP, 8), (TOP + 8, 8), (TOP + 16, 2)):
            scale = inv[p, r : r + size]
            for f in fields:
                start[f - fields[0], p, r : r + size] = (
                    orbs[firsts[f], p, r : r + size] * orbs[seconds[f], p, r : r + size] * scale
                )


def sweep(source, start, coef, fields, row, planes, put):
    values = {}

    def fetch(f, p):
        up = source(f, p, row + 1)
        down = source(f, p, row - 1)
        return source(f, p, row), up - down, up + down

    for f in fields:
        values[f, planes[0] - 1] = fetch(f, planes[0] - 1)
        values[f, planes[0]] = fetch(f, planes[0])
    for p in planes:
        cs = [coef[c, p, row - 8 : row] for c in range(9)]
        for f in fields:
            values[f, p + 1] = fetch(f, p + 1)
            before, diff_before, _ = values.pop((f, p - 1))
            here, diff, both = values[f, p]
            after, diff_after, _ = values[f, p + 1]
            slope = after - before
            up = cs[3] * here + cs[4] * slope + cs[5] * diff
            down = cs[6] * here + cs[7] * slope + cs[8] * diff
            new = start[f - fields[0], p, row : row + 8] + cs[0] * (after + before)
            new = new + cs[1] * both + cs[2] * (diff_after - diff_before)
            put(f, p, new + (pltpu.roll(up, LANES - 1, 1) + pltpu.roll(down, 1, 1)))


def prepare(odd, inv, coef, planes):
    lane = lax.broadcasted_iota(jnp.int32, (8, LANES), 1)
    side = (1 - 2 * odd).astype(jnp.float32)
    for p in planes:
        for r in (0, 8):
            scale = inv[p, 8 + r : 16 + r]
            along = scale * side
            fx, fy, fz, xy, xz, yz = [
                coef[c, p, r : r + 8] * (along if c in (3, 4) else scale) for c in range(6)
            ]
            coef[0, p, r : r + 8] = fx
            coef[1, p, r : r + 8] = fy
            coef[2, p, r : r + 8] = xy
            for at, values, sign in ((3, fz, 1.0), (4, xz, -1.0), (5, yz, -1.0)):
                up = jnp.where(lane == 0, 0.0, pltpu.roll(values, 1, 1))
                down = jnp.where(lane == LANES - 1, 0.0, pltpu.roll(values, LANES - 1, 1))
                coef[at, p, r : r + 8] = up
                coef[at + 3, p, r : r + 8] = sign * down


def take_side(sz, odd, ref, base, first, inv, coef):
    win = sz.window
    for p in range(DEEP):
        inv[base + mirrored(odd, p, DEEP), TOP : TOP + win] = ref[p * win : (p + 1) * win]
    for c in range(6):
        for p in range(sz.edge):
            row = sz.metric_at + (c * sz.edge + p) * sz.inner
            coef[c, base + first + mirrored(odd, p, sz.edge), 0 : sz.inner] = ref[row : row + sz.inner]


def coefs_kernel(sz, near_ref, inv_ref, met_ref, inv, coef):
    odd = lax.rem(lax.axis_index("dom"), 2)
    n = sz.planes
    for p in range(n):
        to = mirrored(odd, p, n)
        inv[to, TOP : TOP + sz.window] = inv_ref[p, 0 : sz.window]
        for c in range(6):
            coef[c, to, 0 : sz.inner] = met_ref[c, p, 0 : sz.inner]
    take_side(sz, odd, near_ref, n, 0, inv, coef)
    prepare(odd, inv, coef, range(n + sz.edge))


class Planes:
    def __init__(self, halo, others):
        self.halo, self.others = halo, others

    def __getitem__(self, at):
        *lead, p, rows = at
        ref, p = (self.halo, p) if p < DEEP else (self.others, p - DEEP)
        return ref[(*lead, p, rows)]


def near_kernel(sz, list_ref, *refs):
    gathered = refs[: sz.groups]
    near_ref, near_rest, inv, coef, state = refs[sz.groups : sz.groups + 5]
    orbs, *refs = refs[sz.groups + 5 :]
    starts, refs = refs[: len(PARTS)], refs[len(PARTS) :]
    every = len(PARTS) * (DEEP - 2)
    levels = refs[:every]
    group = lax.axis_index("orb")
    odd = lax.rem(lax.axis_index("dom"), 2)
    inv, coef = Planes(None, inv), Planes(None, coef)
    fill_own(sz, odd, gathered, orbs)
    fill_side(sz, odd, sz.planes + DEEP, near_ref, near_rest, orbs)

    def batch(parts, base, carry):
        size = parts[-1][1][-1] + 1
        firsts = [list_ref[2 + 3 * (base + f)] for f in range(size)]
        seconds = [list_ref[3 + 3 * (base + f)] for f in range(size)]
        for h, fields in parts:
            fill_start(sz, orbs, inv, starts[h], fields, firsts, seconds, range(DEEP, sz.span))
        for number in range(1, DEEP):
            for h, fields in parts:
                start, low = starts[h], fields[0]
                source = start if number == 1 else levels[h * (DEEP - 2) + number - 2]
                planes = list(range(DEEP + number, sz.span - number))
                for row in (8, 16):

                    def load(f, p, at, source=source, low=low):
                        return source[f - low, p, at : at + 8]

                    def put(f, p, new, row=row, number=number, low=low, h=h):
                        if number < DEEP - 1:
                            levels[h * (DEEP - 2) + number - 1][f - low, p, row : row + 8] = new
                        if p < DEEP + number + 2:
                            state[base + f, number - 1, p - DEEP - number, row : row + 8] = new

                    sweep(load, start, coef, fields, row, planes, put)
        return carry

    full = list_ref[0]
    lax.fori_loop(0, full, lambda i, carry: batch(FULL, i * BATCH, carry), 0)
    lax.fori_loop(0, list_ref[1], lambda i, carry: batch(SHORT, full * BATCH, carry), 0)


def far_kernel(sz, slabs, list_ref, *refs):
    gathered = refs[: sz.groups]
    far_ref, far_rest, inv, coef, state = refs[sz.groups : sz.groups + 5]
    outs = refs[sz.groups + 5 : 2 * sz.groups + 5]
    orbs, inv_far, coef_far, *refs = refs[2 * sz.groups + 5 :]
    totals, refs = refs[:BATCH], refs[BATCH:]
    starts, refs = refs[: len(PARTS)], refs[len(PARTS) :]
    every = len(PARTS) * (DEEP - 1)
    levels = refs[:every]
    group = lax.axis_index("orb")
    slab = lax.axis_index("dom")
    odd = lax.rem(slab, 2)
    n = sz.planes
    take_side(sz, odd, far_ref, 0, 1, inv_far, coef_far)
    inside = jnp.where((slab == 0) | (slab == slabs - 1), 0.0, 1.0)
    for p in range(DEEP):
        inv_far[p, 0:TALL] = inv_far[p, 0:TALL] * inside
    prepare(odd, inv_far, coef_far, range(1, DEEP))
    inv, coef = Planes(inv_far, inv), Planes(coef_far, coef)
    fill_own(sz, odd, gathered, orbs)
    fill_side(sz, odd, 0, far_ref, far_rest, orbs)
    for i in range(sz.orbs):
        for p in range(n):
            for total in totals:
                total[i, p] = jnp.zeros((8, LANES), jnp.float32)

    def batch(parts, base, carry):
        size = parts[-1][1][-1] + 1
        firsts = [list_ref[2 + 3 * (base + f)] for f in range(size)]
        seconds = [list_ref[3 + 3 * (base + f)] for f in range(size)]
        weights = []
        for f in range(size):
            w = list_ref[4 + 3 * (base + f)]
            weights.append(
                (w.astype(jnp.float32), jnp.where(firsts[f] == seconds[f], 0, w).astype(jnp.float32))
            )
        for h, fields in parts:
            fill_start(sz, orbs, inv, starts[h], fields, firsts, seconds, range(DEEP + n))
        for number in range(1, DEEP + 1):
            for h, fields in parts:
                start, low = starts[h], fields[0]
                planes = list(range(number, number + n))

                def load(f, p, at, number=number, start=start, low=low, h=h):
                    if number == 1:
                        return start[f - low, p, at : at + 8]
                    if p < number - 1 + n:
                        return levels[h * (DEEP - 1) + number - 2][f - low, p, at : at + 8]
                    return state[base + f, number - 2, p - (number - 1 + n), at : at + 8]

                if number < DEEP:
                    for row in (8, 16):

                        def put(f, p, new, row=row, number=number, low=low, h=h):
                            levels[h * (DEEP - 1) + number - 1][f - low, p, row : row + 8] = new

                        sweep(load, start, coef, fields, row, planes, put)
                else:
                    row = TOP + DEEP

                    def put(f, p, new, row=row):
                        a, b = firsts[f], seconds[f]
                        q = p - DEEP
                        total = totals[f]
                        total[a, q] = total[a, q] + (weights[f][0] * new) * orbs[b, p, row : row + 8]
                        total[b, q] = total[b, q] + (weights[f][1] * new) * orbs[a, p, row : row + 8]

                    sweep(load, start, coef, fields, row, planes, put)
        return carry

    full = list_ref[0]
    lax.fori_loop(0, full, lambda i, carry: batch(FULL, i * BATCH, carry), 0)
    lax.fori_loop(0, list_ref[1], lambda i, carry: batch(SHORT, full * BATCH, carry), 0)

    for i, s in enumerate(sz.routes):
        for j in range(sz.mine):
            for p in range(n):
                at = mirrored(odd, p, n)
                outs[i][j, p] = sum(total[s * sz.mine + j, at, 0 : sz.rows] for total in totals)


def unpack_kernel(sz, *refs):
    blocks, out_ref = refs[: sz.groups], refs[sz.groups]
    group = lax.axis_index("orb")
    for i, s in enumerate(sz.routes):
        first = jnp.bitwise_xor(group, s) * sz.rows
        if sz.rows % 8 == 0:
            first = pl.multiple_of(first, 8)
        for j in range(sz.mine):
            for p in range(sz.planes):
                out_ref[j, p, pl.ds(first, sz.rows)] = blocks[i][j, p]


def body(groups, slabs, orbitals, face_metric, cross_metric, screen, turn_orbital):
    mine, planes, height, lanes = orbitals.shape
    sz = Sizes(groups, mine, planes, height, turn_orbital.shape[0])
    f32 = jnp.float32
    vmem = pl.BlockSpec(memory_space=pltpu.VMEM)
    hbm = pl.BlockSpec(memory_space=pltpu.HBM)
    smem = pl.BlockSpec(memory_space=pltpu.SMEM)
    params = pltpu.CompilerParams(vmem_limit_bytes=LIMIT)

    packed = pl.pallas_call(
        functools.partial(pack_kernel, sz),
        out_shape=[jax.ShapeDtypeStruct((sz.orb_pack, lanes), f32)] * groups
        + [jax.ShapeDtypeStruct((sz.side_pack, lanes), f32)] * 2
        + [
            jax.ShapeDtypeStruct((planes, 24, lanes), f32),
            jax.ShapeDtypeStruct((6, planes, 16, lanes), f32),
        ],
        in_specs=[hbm] * 4,
        out_specs=[vmem] * (groups + 4),
        scratch_shapes=[
            pltpu.VMEM((mine, planes, height + 16, lanes), f32),
            pltpu.VMEM((7, planes, height + 16, lanes), f32),
            pltpu.VMEM((mine, planes, height, lanes), f32),
            pltpu.VMEM((3, planes, height, lanes), f32),
            pltpu.VMEM((3, planes, height, lanes), f32),
            pltpu.VMEM((planes, height, lanes), f32),
            pltpu.SemaphoreType.DMA((4,)),
        ],
        compiler_params=params,
        name="pack",
    )(*[pltpu.with_memory_space_constraint(x, pltpu.HBM) for x in (orbitals, face_metric, cross_metric, screen)])
    pieces = packed[:groups]
    far, near, inverse, metric = packed[groups:]

    def swap(x, s):
        return lax.ppermute(x, "orb", [(i, i ^ s) for i in range(groups)])

    to_near = [(i, i ^ 1) for i in range(slabs)]
    to_far = []
    for g in range(groups):
        to_far += [(g * slabs + i, g * slabs + ((i + 1) ^ 1) - 1) for i in range(1, slabs - 1)]
        to_far += [(g * slabs + i, (g ^ 1) * slabs + i) for i in (0, slabs - 1)]
    gathered = [pieces[0]] + [swap(piece, s) for piece, s in zip(pieces[1:], sz.routes[1:])]
    far_side = lax.ppermute(far, ("orb", "dom"), to_far)
    near_side = lax.ppermute(near, "dom", to_near)
    turns = sz.turns
    most = turns * sz.orbs - turns * (turns - 1) // 2
    most = -(-most // BATCH) * BATCH
    room = turns * sz.orbs + BATCH
    which = pltpu.with_memory_space_constraint(turn_orbital, pltpu.HBM)
    points = sz.rows * planes * lanes
    pairs = pl.pallas_call(
        functools.partial(list_kernel, sz),
        out_shape=jax.ShapeDtypeStruct((2 + 3 * room,), jnp.int32),
        in_specs=[hbm],
        out_specs=smem,
        scratch_shapes=[
            pltpu.SMEM((sz.orbs,), jnp.int32),
            pltpu.SMEM((sz.orbs,), jnp.int32),
            pltpu.SMEM((turns,), jnp.int32),
            pltpu.SemaphoreType.DMA(()),
        ],
        compiler_params=params,
        name="pairs",
    )(which)
    inverse, coefs = pl.pallas_call(
        functools.partial(coefs_kernel, sz),
        out_shape=[
            jax.ShapeDtypeStruct((planes + DEEP, TALL, lanes), f32),
            jax.ShapeDtypeStruct((9, planes + DEEP, 16, lanes), f32),
        ],
        in_specs=[vmem] * 3,
        out_specs=[vmem] * 2,
        compiler_params=params,
        cost_estimate=pl.CostEstimate(flops=50 * points, bytes_accessed=2_500_000, transcendentals=0),
        name="coefs",
    )(near_side, inverse, metric)
    *gathered, pairs, inverse, coefs = lax.optimization_barrier((*gathered, pairs, inverse, coefs))
    rest = jnp.concatenate(gathered[1:], axis=0)
    far_rest = lax.ppermute(rest, ("orb", "dom"), to_far)
    near_rest = lax.ppermute(rest, "dom", to_near)

    field = [pltpu.VMEM((len(fields), sz.span, TALL, lanes), f32) for fields in PARTS]
    orbital_windows = pltpu.VMEM((sz.orbs, sz.span, TALL, lanes), f32)
    state = pl.pallas_call(
        functools.partial(near_kernel, sz),
        out_shape=jax.ShapeDtypeStruct((most, DEEP - 1, 2, TALL, lanes), f32),
        in_specs=[smem] + [vmem] * (groups + 4),
        out_specs=vmem,
        scratch_shapes=[orbital_windows] + field + [x for x in field for _ in range(DEEP - 2)],
        compiler_params=params,
        cost_estimate=pl.CostEstimate(flops=200 * most * points, bytes_accessed=20_000_000, transcendentals=0),
        name="near",
    )(pairs, *gathered, near_side, near_rest, inverse, coefs)
    shares = pl.pallas_call(
        functools.partial(far_kernel, sz, slabs),
        out_shape=[jax.ShapeDtypeStruct((mine, planes, sz.rows, lanes), f32)] * groups,
        in_specs=[smem] + [vmem] * (groups + 5),
        out_specs=[vmem] * groups,
        scratch_shapes=[
            orbital_windows,
            pltpu.VMEM((DEEP, TALL, lanes), f32),
            pltpu.VMEM((9, DEEP, 16, lanes), f32),
        ]
        + [pltpu.VMEM((sz.orbs, planes, 8, lanes), f32)] * BATCH
        + field
        + [x for x in field for _ in range(DEEP - 1)]
       ,
        compiler_params=params,
        name="far",
    )(pairs, *gathered, far_side, far_rest, inverse, coefs, state)
    blocks = [shares[0]] + [swap(share, s) for share, s in zip(shares[1:], sz.routes[1:])]
    return pl.pallas_call(
        functools.partial(unpack_kernel, sz),
        out_shape=jax.ShapeDtypeStruct((mine, planes, height, lanes), f32),
        in_specs=[vmem] * groups,
        out_specs=vmem,
        compiler_params=params,
        name="unpack",
    )(*blocks)


def solution(mesh):
    in_specs = (
        P("orb", "dom", None, None),
        P(None, "dom", None, None),
        P(None, "dom", None, None),
        P("dom", None, None),
        P(),
    )
    out_specs = P("orb", "dom", None, None)
    return jax.shard_map(
        functools.partial(body, mesh.shape["orb"], mesh.shape["dom"]),
        mesh=mesh,
        in_specs=in_specs,
        out_specs=out_specs,
        check_vma=False,
    )
```
